512 devices in a mesh: row: 64 (over z_lo, x, y), col: 8 (over z_hi, core).
Axes of the slice: x: 4, y: 8, z: 8 (z_hi: 4, z_lo: 2; z = z_hi * 2 + z_lo), core: 2. Of those that a mesh axis runs over, the one named last changes fastest.
Arguments:
- slab: float32 [4096, 8192], P('row', 'col')
- pairing: int32 [2, 8], replicated, may hold values from 0 to 2, as said below
Outputs:
- rotated: float32 [4096, 8192], P('row', 'col')
The draws below stay inside these ranges and needn't reach their ends.
Inputs may be any that keep to these rules, and one draw needn't show every extreme that they name: `pairing`: each entry names one of the three pairings of a group's slots.
All inputs are finite; a program needn't handle non-finite values.
Results may differ from the reference program's by a relative error of at most 0.00045.
Values sent between devices are 32-bit elements; how exact they have to be, the bound alone decides.
No kernel may reach another device: no remote copies, remote signals or barrier semaphores. Data moves between devices by JAX's collectives and lax.ppermute only.
A program may use at most 64 MiB of HBM per device.

```python
import math
import jax
import jax.numpy as jnp
from jax import lax

BLOCK = 256
ROUNDS = 2
GROUPS = 8
ROWS = 4096
COLS = 8192


def draw_slab(key, part):
    key = jax.random.fold_in(key, 11)
    keys = jax.random.split(key, 3)
    low = math.log(0.3)
    high = math.log(3.0)
    row_scale = jnp.exp(jax.random.uniform(keys[1], (ROWS, 1), jnp.float32, low, high))
    col_scale = jnp.exp(jax.random.uniform(keys[2], (1, COLS), jnp.float32, low, high))
    base = jax.random.normal(keys[0], (ROWS, COLS), jnp.float32)
    return (base * row_scale * col_scale).astype(jnp.float32)


def draw_pairing(key, part):
    key = jax.random.fold_in(key, 23)
    values = jax.random.randint(key, (ROUNDS, GROUPS), 0, 3, jnp.int32)
    values = values.at[0, 0].set(0)
    values = values.at[ROUNDS - 1, GROUPS - 1].set(2)
    return values.astype(jnp.int32)


def setup_inputs(seed: int = 0) -> dict:
    splits = jax.random.split(jax.random.key(seed), 3)
    slab = draw_slab(jax.random.fold_in(splits[2], 71), 0)
    pairing = draw_pairing(jax.random.fold_in(splits[2], 71), 0)
    return dict(slab=slab, pairing=pairing)


EPS = 1e-06
ORDERS = ((0, 1, 2, 3), (0, 2, 1, 3), (0, 3, 1, 2))
RESTORE = ((0, 1, 2, 3), (0, 2, 1, 3), (0, 2, 3, 1))

def arrange(blocks, which, tables):
    branches = [lambda b, order=order: jnp.stack([b[:, i] for i in order], axis=1) for order in tables]
    return lax.switch(which, branches, blocks)

def inverse_of(matrix, eye):
    factor = jnp.linalg.cholesky(matrix)
    lower_inv = lax.linalg.triangular_solve(factor, eye, left_side=True, lower=True)
    return jnp.dot(lower_inv.T, lower_inv, precision=lax.Precision.HIGHEST)

def rotate(first, second, cross, norm_first, norm_second, eye):
    high = lax.Precision.HIGHEST
    coupling = cross * lax.rsqrt(norm_first + EPS)[:, None] * lax.rsqrt(norm_second + EPS)[None, :]
    p_inv = inverse_of(eye + jnp.dot(coupling, coupling.T, precision=high), eye)
    q_inv = inverse_of(eye + jnp.dot(coupling.T, coupling, precision=high), eye)
    top = jnp.concatenate([2.0 * p_inv - eye, 2.0 * jnp.dot(p_inv, coupling, precision=high)], axis=1)
    bottom = jnp.concatenate([-2.0 * jnp.dot(q_inv, coupling.T, precision=high), 2.0 * q_inv - eye], axis=1)
    rotation = jnp.concatenate([top, bottom], axis=0)
    joined = jnp.concatenate([first, second], axis=1)
    result = jnp.dot(joined, rotation, precision=high)
    width = first.shape[1]
    return (result[:, :width], result[:, width:])

def one_group(item):
    group_blocks, which = item
    eye = jnp.eye(BLOCK, dtype=jnp.float32)
    high = lax.Precision.HIGHEST
    ordered = arrange(group_blocks, which, ORDERS)
    outputs = []
    for pair in range(2):
        first = ordered[:, 2 * pair]
        second = ordered[:, 2 * pair + 1]
        cross = jnp.dot(first.T, second, precision=high)
        outputs.extend(rotate(first, second, cross, lax.optimization_barrier(jnp.sum(first * first, axis=0)), lax.optimization_barrier(jnp.sum(second * second, axis=0)), eye))
    stacked = jnp.stack(outputs, axis=1)
    return arrange(stacked, which, RESTORE)

def reference(slab, pairing):
    blocks = slab.reshape(ROWS, GROUPS, 4, BLOCK).transpose(1, 0, 2, 3)
    for step in range(ROUNDS):
        blocks = lax.map(one_group, (blocks, pairing[step]))
        if step + 1 < ROUNDS:
            ahead = jnp.roll(blocks[:, :, 1], 1, axis=0)
            behind = jnp.roll(blocks[:, :, 3], -1, axis=0)
            blocks = jnp.stack([blocks[:, :, 0], ahead, blocks[:, :, 2], behind], axis=2)
    return blocks.transpose(1, 0, 2, 3).reshape(ROWS, 4 * GROUPS * BLOCK)
```

```python
import functools
import math

import jax
import jax.numpy as jnp
from jax import lax
from jax.experimental import pallas as pl
from jax.experimental.pallas import tpu as pltpu
from jax.sharding import Mesh, PartitionSpec as P

EPS = 1e-06
WIDTH = 256
HALF = 128
ROWS = 64
CHUNKS = 16
PART = WIDTH // CHUNKS
NORMS = 4 * PART
OUTER = ("z_lo", "x", "y_lo")
RING = ("y_hi",)
COL = ("z_hi", "core")

NT = (((1,), (1,)), ((), ()))
NN = (((1,), (0,)), ((), ()))
TN = (((0,), (0,)), ((), ()))


TOLERANCE = 2e-6


def step_table():
    table = []
    steps = 32
    while not table or table[-1][1] < 70000.0:
        low, high = 0.0, 1e6
        for _ in range(80):
            b = 0.5 * (low + high)
            root = 2.0 * math.sqrt(1.0 + b) / (2.0 + b)
            rho = b / (2.0 + b) / (1.0 + root)
            error = rho ** (steps + 1) * (1.0 + (steps + 1) * root)
            low, high = (b, high) if error < TOLERANCE else (low, b)
        table.append((steps, low))
        steps = (steps * 5) // 4
    return fourth(table)


def squaring_table():
    table = []
    for count in range(1, 7):
        mu = TOLERANCE ** (0.5 ** (count + 2))
        table.append((count, 2.0 * mu / (1.0 - mu)))
    return fourth(table)


def fourth(table):
    return [(count, (limit / 1.001) ** 4) for count, limit in table]


def count_of(bound, table):
    count = table[0][0]
    for (_, limit), (more, _) in zip(table[:-1], table[1:]):
        count = jnp.where(bound > limit, more, count)
    return count


STEPS = step_table()
SQUARINGS = squaring_table()


def halves(a):
    high = a.astype(jnp.bfloat16)
    return high, (a - high.astype(jnp.float32)).astype(jnp.bfloat16)


def stack(a, b):
    return tuple(jnp.concatenate(p, axis=0) for p in zip(a, b))


def dot3(a, b, dims):
    ah, al = a
    bh, bl = b
    dot = lambda u, v: lax.dot_general(u, v, dims, preferred_element_type=jnp.float32)
    return dot(ah, bh) + (dot(ah, bl) + dot(al, bh))


def slots_of(which):
    first_b = jnp.where(which == 0, 2, 1)
    second_b = jnp.where(which == 2, 2, 3)
    return ((0, which + 1), (first_b, second_b))


def pick(pairing_ref, step):
    return pairing_ref[step, lax.axis_index(COL)]


def load_blocks(refs, blocks):
    for s in range(4):
        blocks[s] = refs[0][:, s * WIDTH : (s + 1) * WIDTH] if len(refs) == 1 else refs[s][...]


def gram_kernel(step, pairing_ref, *refs):
    *ins, out, blocks = refs
    load_blocks(ins, blocks)
    for c in range(1, CHUNKS):
        out[c, NORMS:] = jnp.zeros((8, HALF), jnp.float32)
    for pair, (f, s) in enumerate(slots_of(pick(pairing_ref, step))):
        x = blocks[f]
        y = blocks[s]
        cross = dot3(halves(x), halves(y), TN)
        for side, block in enumerate((x, y)):
            norm = jnp.sum(block * block, axis=0, keepdims=True)
            for h in range(2):
                row = NORMS + 4 * pair + 2 * side + h
                out[0, row : row + 1] = norm[:, h * HALF : (h + 1) * HALF]
        for h in range(2):
            start = (2 * pair + h) * PART
            half = cross[:, h * HALF : (h + 1) * HALF]
            out[:, start : start + PART, :] = half.reshape(CHUNKS, PART, HALF)


def sum_kernel(parts, out):
    total = parts[0]
    for c in range(1, parts.shape[0]):
        total = total + parts[c]
    for c in range(out.shape[0]):
        out[c] = total


def turn_kernel(step, pairing_ref, gram, *refs):
    count = 1 if step == 0 else 4
    ins, outs, (blocks, coupling, powers, solved) = refs[:count], refs[count:-4], refs[-4:]
    load_blocks(ins, blocks)
    pairs = slots_of(pick(pairing_ref, step))
    scale = lax.rsqrt(gram[0, NORMS:] + EPS)
    scale_t = scale.T
    xs, ys, cs, ms, ts, starts, squares = [], [], [], [], [], [], []
    bound = None
    for pair, (f, s) in enumerate(pairs):
        x = blocks[f]
        y = blocks[s]
        row = 4 * pair
        down = jnp.concatenate([scale_t[:, row : row + 1], scale_t[:, row + 1 : row + 2]], axis=0)
        sides = []
        for h in range(2):
            start = (2 * pair + h) * PART
            half = gram[:, start : start + PART, :].reshape(WIDTH, HALF)
            sides.append(half * down * scale[row + 2 + h : row + 3 + h])
        coupling[pair] = jnp.concatenate(sides, axis=1)
        c = halves(coupling[pair])
        both = dot3(stack(halves(y), c), c, NT)
        t = x - both[:ROWS]
        m = both[ROWS:]
        mh = halves(m)
        both = dot3(stack(halves(t), mh), mh, NN)
        square = both[ROWS:]
        most = jnp.sum(square * square)
        bound = most if bound is None else jnp.maximum(bound, most)
        xs.append(x)
        ys.append(y)
        cs.append(c)
        ms.append(m)
        ts.append(t)
        starts.append(both[:ROWS])
        squares.append(square)
    b = jnp.sqrt(jnp.sqrt(jnp.full((8, 128), bound, jnp.float32)))[:1, :1] * 1.001

    @pl.when(bound <= SQUARINGS[-1][1])
    def _():
        relax = 2.0 / (2.0 + b)
        keep = 0.5 * b * relax
        diagonal = lax.broadcasted_iota(jnp.int32, (WIDTH, WIDTH), 0) == lax.broadcasted_iota(
            jnp.int32, (WIDTH, WIDTH), 1
        )
        for pair in range(2):
            off = (relax * relax) * squares[pair] - (2.0 * keep * relax) * ms[pair]
            powers[pair] = jnp.where(diagonal, off + keep * keep, off)
            solved[pair] = relax * ((1.0 + keep) * ts[pair] - relax * starts[pair])

        def body(_, carry):
            for pair in range(2):
                z = solved[pair]
                r = halves(powers[pair])
                both = dot3(stack(halves(z), r), r, NN)
                solved[pair] = z + both[:ROWS]
                powers[pair] = both[ROWS:]
            return carry

        lax.fori_loop(0, count_of(bound, SQUARINGS), body, 0)
        for pair, ((f, s), x, y, c) in enumerate(zip(pairs, xs, ys, cs)):
            z = solved[pair]
            z = z + dot3(halves(z), halves(powers[pair]), NN)
            blocks[f] = 2.0 * z - x
            blocks[s] = y + 2.0 * dot3(halves(z), c, NN)

    @pl.when(bound > SQUARINGS[-1][1])
    def _():
        dot = functools.partial(
            lax.dot_general, precision=lax.Precision.HIGHEST, preferred_element_type=jnp.float32
        )
        relax = 2.0 / (2.0 + b)
        omega = 2.0 / (1.0 + relax * jnp.sqrt(1.0 + b))
        gain = omega * relax
        for pair, (f, s) in enumerate(pairs):
            x = blocks[f]
            y = blocks[s]
            c = coupling[pair]
            t = x - dot(y, c, NT)
            powers[pair] = dot(c, c, NT)

            def body(_, carry):
                z, before = carry
                residual = t - z - dot(z, powers[pair], NN)
                return before + omega * (z - before) + gain * residual, z

            z, _ = lax.fori_loop(0, count_of(bound, STEPS), body, (relax * t, jnp.zeros_like(t)))
            blocks[f] = 2.0 * z - x
            blocks[s] = y + 2.0 * dot(z, c, NN)

    for s in range(4):
        if len(outs) == 1:
            outs[0][:, s * WIDTH : (s + 1) * WIDTH] = blocks[s]
        else:
            outs[s][...] = blocks[s]


SMEM = pl.BlockSpec(memory_space=pltpu.SMEM)
VMEM = pl.BlockSpec(memory_space=pltpu.VMEM)
BLOCKS = pltpu.VMEM((4, ROWS, WIDTH), jnp.float32)
PARAMS = pltpu.CompilerParams(vmem_limit_bytes=8 * 2**20)


def shape(*sizes):
    return jax.ShapeDtypeStruct(sizes, jnp.float32)


def gram_of(step, pairing, ins):
    return pl.pallas_call(
        lambda *refs: gram_kernel(step, *refs),
        out_shape=shape(CHUNKS, NORMS + 8, HALF),
        in_specs=[SMEM] + [VMEM] * len(ins),
        out_specs=VMEM,
        scratch_shapes=[BLOCKS],
        compiler_params=PARAMS,
        name="gram",
    )(pairing, *ins)


def add_up(parts, copies):
    return pl.pallas_call(
        sum_kernel,
        out_shape=shape(copies, *parts.shape[1:]),
        in_specs=[VMEM],
        out_specs=VMEM,
        compiler_params=PARAMS,
        name="add_up",
    )(parts)


def turn(step, pairing, gram, ins):
    outs = [shape(ROWS, WIDTH)] * 4 if step == 0 else shape(ROWS, 4 * WIDTH)
    return pl.pallas_call(
        lambda *refs: turn_kernel(step, *refs),
        out_shape=outs,
        in_specs=[SMEM] + [VMEM] * (1 + len(ins)),
        out_specs=[VMEM] * 4 if step == 0 else VMEM,
        scratch_shapes=[
            BLOCKS,
            pltpu.VMEM((2, WIDTH, WIDTH), jnp.float32),
            pltpu.VMEM((2, WIDTH, WIDTH), jnp.float32),
            pltpu.VMEM((2, ROWS, WIDTH), jnp.float32),
        ],
        compiler_params=PARAMS,
        name="turn",
    )(pairing, gram, *ins)


def whole(parts):
    parts = add_up(lax.all_to_all(parts, OUTER, 0, 0), lax.axis_size(RING))
    parts = add_up(lax.all_to_all(parts, RING, 0, 0), CHUNKS)
    return lax.all_to_all(parts, OUTER, 0, 0)


def local(slab, pairing):
    ins = (slab,)
    gram = whole(gram_of(0, pairing, ins))
    stay, ahead, wait, behind = turn(0, pairing, gram, ins)
    ahead = lax.ppermute(ahead, COL, [(i, (i + 1) % 8) for i in range(8)])
    behind = lax.ppermute(behind, COL, [(i, (i - 1) % 8) for i in range(8)])
    ins = (stay, ahead, wait, behind)
    gram = whole(gram_of(1, pairing, ins))
    return turn(1, pairing, gram, ins)


def solution(mesh):
    names = ("z_lo", "x", "y_hi", "y_lo", "z_hi", "core")
    fine = Mesh(mesh.devices.reshape(2, 4, 4, 2, 4, 2), names)
    spec = P(names[:4], COL)
    return jax.shard_map(local, mesh=fine, in_specs=(spec, P()), out_specs=spec, check_vma=False)
```

```python
import functools
import math

import jax
import jax.numpy as jnp
from jax import lax
from jax.experimental import pallas as pl
from jax.experimental.pallas import tpu as pltpu
from jax.sharding import Mesh, PartitionSpec as P

EPS = 1e-06
WIDTH = 256
HALF = 128
ROWS = 64
CHUNKS = 16
PART = WIDTH // CHUNKS
NORMS = 4 * PART
OUTER = ("z_lo", "x", "y_lo")
RING = ("y_hi",)
COL = ("z_hi", "core")
CORE = "core"

NT = (((1,), (1,)), ((), ()))
NN = (((1,), (0,)), ((), ()))
TN = (((0,), (0,)), ((), ()))


TOLERANCE = 2e-6
CUBIC_TOLERANCE = 1e-5


def step_table():
    table = []
    steps = 32
    while not table or table[-1][1] < 70000.0:
        low, high = 0.0, 1e6
        for _ in range(80):
            b = 0.5 * (low + high)
            root = 2.0 * math.sqrt(1.0 + b) / (2.0 + b)
            rho = b / (2.0 + b) / (1.0 + root)
            error = rho ** (steps + 1) * (1.0 + (steps + 1) * root)
            low, high = (b, high) if error < TOLERANCE else (low, b)
        table.append((steps, low))
        steps = (steps * 5) // 4
    return fourth(table)


def squaring_table():
    rho = (0.5 * CUBIC_TOLERANCE) ** 0.25
    top = 4.0 * rho / (1.0 + rho) ** 2
    table = []
    for count in range(1, 7):
        mu = top ** (0.5**count)
        table.append((count, 2.0 * mu / (1.0 - mu)))
    return fourth(table)


def fourth(table):
    return [(count, (limit / 1.001) ** 4) for count, limit in table]


def count_of(bound, table):
    count = table[0][0]
    for (_, limit), (more, _) in zip(table[:-1], table[1:]):
        count = jnp.where(bound > limit, more, count)
    return count


STEPS = step_table()
SQUARINGS = squaring_table()


def halves(a):
    high = a.astype(jnp.bfloat16)
    return high, (a - high.astype(jnp.float32)).astype(jnp.bfloat16)


def dots3(operands, dims):
    dot = lambda u, v: lax.dot_general(u, v, dims, preferred_element_type=jnp.float32)
    tops = [dot(a[0], b[0]) for a, b in operands]
    lows = [dot(a[0], b[1]) for a, b in operands]
    highs = [dot(a[1], b[0]) for a, b in operands]
    return [t + (l + h) for t, l, h in zip(tops, lows, highs)]


def slots_of(which):
    first_b = jnp.where(which == 0, 2, 1)
    second_b = jnp.where(which == 2, 2, 3)
    return ((0, which + 1), (first_b, second_b))


def pick(pairing_ref, step):
    row = pairing_ref[step : step + 1, :]
    mine = lax.broadcasted_iota(jnp.int32, row.shape, 1) == lax.axis_index(COL)
    return jnp.max(jnp.where(mine, row, 0).astype(jnp.float32)).astype(jnp.int32)


def load_blocks(refs, blocks):
    if len(refs) == 1:
        for s in range(4):
            blocks[s] = refs[0][:, s * WIDTH : (s + 1) * WIDTH]
    else:
        low, high, near, far = refs
        core = lax.axis_index(CORE)
        blocks[0] = low[...]
        blocks[2] = high[...]
        blocks[3 - 2 * core] = near[1 - core]
        blocks[1 + 2 * core] = far[...]


def fetch_gram_kernel(pairing_hbm, slab_hbm, out, blocks, pairing, slab, sems):
    copies = [
        pltpu.make_async_copy(pairing_hbm, pairing, sems.at[0]),
        pltpu.make_async_copy(slab_hbm, slab, sems.at[1]),
    ]
    for copy in copies:
        copy.start()
    for copy in copies:
        copy.wait()
    gram_kernel(0, pairing, slab, out, blocks)


def gram_kernel(step, pairing_ref, *refs):
    *ins, out, blocks = refs
    load_blocks(ins, blocks)
    for c in range(1, CHUNKS):
        out[c, NORMS:] = jnp.zeros((8, HALF), jnp.float32)
    for pair, (f, s) in enumerate(slots_of(pick(pairing_ref, step))):
        x = blocks[f]
        y = blocks[s]
        xh, xl = halves(x)
        yh, yl = halves(y)
        cross = lax.dot_general(
            jnp.concatenate([xh, xh, xl], axis=0),
            jnp.concatenate([yh, yl, yh], axis=0),
            TN,
            preferred_element_type=jnp.float32,
        )
        for side, block in enumerate((x, y)):
            norm = jnp.sum(block * block, axis=0, keepdims=True)
            for h in range(2):
                row = NORMS + 4 * pair + 2 * side + h
                out[0, row : row + 1] = norm[:, h * HALF : (h + 1) * HALF]
        for h in range(2):
            start = (2 * pair + h) * PART
            half = cross[:, h * HALF : (h + 1) * HALF]
            out[:, start : start + PART, :] = half.reshape(CHUNKS, PART, HALF)


def sum_kernel(parts, out):
    total = parts[0]
    for c in range(1, parts.shape[0]):
        total = total + parts[c]
    for c in range(out.shape[0]):
        out[c] = total


def turn_kernel(step, pairing_ref, gram, *refs):
    count = 1 if step == 0 else 4
    ins, outs, (blocks, coupling, powers, solved) = refs[:count], refs[count:-4], refs[-4:]
    load_blocks(ins, blocks)
    pairs = slots_of(pick(pairing_ref, step))
    scale = lax.rsqrt(gram[0, NORMS:] + EPS)
    scale_t = scale.T
    xs, ys, cs, ms, ts, starts, m_squares = [], [], [], [], [], [], []
    bound = None
    for pair, (f, s) in enumerate(pairs):
        x = blocks[f]
        y = blocks[s]
        row = 4 * pair
        down = jnp.concatenate([scale_t[:, row : row + 1], scale_t[:, row + 1 : row + 2]], axis=0)
        sides = []
        for h in range(2):
            start = (2 * pair + h) * PART
            half = gram[:, start : start + PART, :].reshape(WIDTH, HALF)
            sides.append(half * down * scale[row + 2 + h : row + 3 + h])
        coupling[pair] = jnp.concatenate(sides, axis=1)
        cs.append(halves(coupling[pair]))
        xs.append(x)
        ys.append(y)
    ms = dots3([(c, c) for c in cs], NT)
    ts = [x - yc for x, yc in zip(xs, dots3([(halves(y), c) for y, c in zip(ys, cs)], NT))]
    splits = [halves(m) for m in ms]
    m_squares = dots3([(m, m) for m in splits], NN)
    starts = dots3([(halves(t), m) for t, m in zip(ts, splits)], NN)
    for pair in range(2):
        most = jnp.sum(m_squares[pair] * m_squares[pair])
        bound = most if bound is None else jnp.maximum(bound, most)
    b = jnp.sqrt(jnp.sqrt(jnp.full((8, 128), bound, jnp.float32)))[:1, :1] * 1.001

    @pl.when(bound <= SQUARINGS[-1][1])
    def _():
        relax = 2.0 / (2.0 + b)
        keep = 0.5 * b * relax
        diagonal = lax.broadcasted_iota(jnp.int32, (WIDTH, WIDTH), 0) == lax.broadcasted_iota(
            jnp.int32, (WIDTH, WIDTH), 1
        )
        for pair in range(2):
            off = (relax * relax) * m_squares[pair] - (2.0 * keep * relax) * ms[pair]
            powers[pair] = jnp.where(diagonal, off + keep * keep, off)
            solved[pair] = relax * ((1.0 + keep) * ts[pair] - relax * starts[pair])

        def body(_, carry):
            zs = [solved[pair] for pair in range(2)]
            rs = [halves(powers[pair]) for pair in range(2)]
            zrs = dots3([(halves(z), r) for z, r in zip(zs, rs)], NN)
            squares = dots3([(r, r) for r in rs], NN)
            zs = [z + zr for z, zr in zip(zs, zrs)]
            for pair in range(2):
                solved[pair] = zs[pair]
                powers[pair] = squares[pair]
            return carry

        count = count_of(bound, SQUARINGS)
        lax.fori_loop(1, count, body, 0)
        top = keep
        for index in range(len(SQUARINGS)):
            top = jnp.where(count > index, top * top, top)
        third = 1.0
        second = third - 2.0 * top
        first = second + 1.25 * top * top
        zeroth = first - 0.25 * top * top * top
        unit = 1.0 / (zeroth + top * top * top * top * (1.0 / 128.0))
        zs = [solved[pair] for pair in range(2)]
        rs = [halves(powers[pair]) for pair in range(2)]
        squares = dots3([(r, r) for r in rs], NN)
        zrs = dots3([(halves(z), r) for z, r in zip(zs, rs)], NN)
        highs = [(unit * second) * z + unit * zr for z, zr in zip(zs, zrs)]
        tops = dots3([(halves(h), halves(q)) for h, q in zip(highs, squares)], NN)
        zs = [(unit * zeroth) * z + (unit * first) * zr + t for z, zr, t in zip(zs, zrs, tops)]
        zcs = dots3([(halves(z), c) for z, c in zip(zs, cs)], NN)
        for (f, s), x, y, z, zc in zip(pairs, xs, ys, zs, zcs):
            blocks[f] = 2.0 * z - x
            blocks[s] = y + 2.0 * zc

    @pl.when(bound > SQUARINGS[-1][1])
    def _():
        dot = functools.partial(
            lax.dot_general, precision=lax.Precision.HIGHEST, preferred_element_type=jnp.float32
        )
        relax = 2.0 / (2.0 + b)
        omega = 2.0 / (1.0 + relax * jnp.sqrt(1.0 + b))
        gain = omega * relax
        for pair, (f, s) in enumerate(pairs):
            x = blocks[f]
            y = blocks[s]
            c = coupling[pair]
            t = x - dot(y, c, NT)
            powers[pair] = dot(c, c, NT)

            def body(_, carry):
                z, before = carry
                residual = t - z - dot(z, powers[pair], NN)
                return before + omega * (z - before) + gain * residual, z

            z, _ = lax.fori_loop(0, count_of(bound, STEPS), body, (relax * t, jnp.zeros_like(t)))
            blocks[f] = 2.0 * z - x
            blocks[s] = y + 2.0 * dot(z, c, NN)

    if len(outs) == 1:
        for s in range(4):
            outs[0][:, s * WIDTH : (s + 1) * WIDTH] = blocks[s]
    else:
        low, high, near, far = outs
        core = lax.axis_index(CORE)
        low[...] = blocks[0]
        high[...] = blocks[2]
        near[0] = near[1] = blocks[1 + 2 * core]
        far[...] = blocks[3 - 2 * core]


VMEM = pl.BlockSpec(memory_space=pltpu.VMEM)
HBM = pl.BlockSpec(memory_space=pltpu.HBM)
BLOCKS = pltpu.VMEM((4, ROWS, WIDTH), jnp.float32)
PARAMS = pltpu.CompilerParams(vmem_limit_bytes=8 * 2**20)


def shape(*sizes):
    return jax.ShapeDtypeStruct(sizes, jnp.float32)


def first_gram(pairing, slab):
    return pl.pallas_call(
        fetch_gram_kernel,
        out_shape=shape(CHUNKS, NORMS + 8, HALF),
        in_specs=[HBM] * 2,
        out_specs=VMEM,
        scratch_shapes=[
            BLOCKS,
            pltpu.VMEM(pairing.shape, pairing.dtype),
            pltpu.VMEM(slab.shape, slab.dtype),
            pltpu.SemaphoreType.DMA((2,)),
        ],
        compiler_params=PARAMS,
        name="first_gram",
    )(pairing, slab)


def gram_of(step, pairing, ins):
    return pl.pallas_call(
        lambda *refs: gram_kernel(step, *refs),
        out_shape=shape(CHUNKS, NORMS + 8, HALF),
        in_specs=[VMEM] * (1 + len(ins)),
        out_specs=VMEM,
        scratch_shapes=[BLOCKS],
        compiler_params=PARAMS,
        name="gram",
    )(pairing, *ins)


def add_up(parts, copies):
    return pl.pallas_call(
        sum_kernel,
        out_shape=shape(copies, *parts.shape[1:]),
        in_specs=[VMEM],
        out_specs=VMEM,
        compiler_params=PARAMS,
        name="add_up",
    )(parts)


def turn(step, pairing, gram, ins):
    outs = [shape(ROWS, WIDTH)] * 2 + [shape(2, ROWS, WIDTH), shape(ROWS, WIDTH)] if step == 0 else shape(ROWS, 4 * WIDTH)
    return pl.pallas_call(
        lambda *refs: turn_kernel(step, *refs),
        out_shape=outs,
        in_specs=[VMEM] * (2 + len(ins)),
        out_specs=[VMEM] * 4 if step == 0 else VMEM,
        scratch_shapes=[
            BLOCKS,
            pltpu.VMEM((2, WIDTH, WIDTH), jnp.float32),
            pltpu.VMEM((2, WIDTH, WIDTH), jnp.float32),
            pltpu.VMEM((2, ROWS, WIDTH), jnp.float32),
        ],
        compiler_params=PARAMS,
        name="turn",
    )(pairing, gram, *ins)


def whole(parts):
    parts = add_up(lax.all_to_all(parts, OUTER, 0, 0), lax.axis_size(RING))
    parts = add_up(lax.all_to_all(parts, RING, 0, 0), CHUNKS)
    return lax.all_to_all(parts, OUTER, 0, 0)


def local(slab, pairing):
    ins = (slab,)
    gram = whole(first_gram(pairing, slab))
    low, high, near, far = turn(0, pairing, gram, ins)
    far = lax.ppermute(far, COL, [(i, (i + 1 if i % 2 else i - 1) % 8) for i in range(8)])
    near = lax.all_to_all(near, CORE, 0, 0)
    ins = (low, high, near, far)
    gram = whole(gram_of(1, pairing, ins))
    return turn(1, pairing, gram, ins)


def solution(mesh):
    names = ("z_lo", "x", "y_hi", "y_lo", "z_hi", "core")
    fine = Mesh(mesh.devices.reshape(2, 4, 4, 2, 4, 2), names)
    spec = P(names[:4], COL)
    return jax.shard_map(local, mesh=fine, in_specs=(spec, P()), out_specs=spec, check_vma=False)
```

```python
import functools
import math

import jax
import jax.numpy as jnp
from jax import lax
from jax.experimental import pallas as pl
from jax.experimental.pallas import tpu as pltpu
from jax.sharding import Mesh, PartitionSpec as P

EPS = 1e-06
WIDTH = 256
HALF = 128
ROWS = 64
CHUNKS = 16
PART = WIDTH // CHUNKS
NORMS = 4 * PART
OUTER = ("z_lo", "x", "y_lo")
RING = ("y_hi",)
COL = ("z_hi", "core")
CORE = "core"

NT = (((1,), (1,)), ((), ()))
NN = (((1,), (0,)), ((), ()))
TN = (((0,), (0,)), ((), ()))


TOLERANCE = 2e-6
CUBIC_TOLERANCE = 1e-5


def step_table():
    table = []
    steps = 32
    while not table or table[-1][1] < 70000.0:
        low, high = 0.0, 1e6
        for _ in range(80):
            b = 0.5 * (low + high)
            root = 2.0 * math.sqrt(1.0 + b) / (2.0 + b)
            rho = b / (2.0 + b) / (1.0 + root)
            error = rho ** (steps + 1) * (1.0 + (steps + 1) * root)
            low, high = (b, high) if error < TOLERANCE else (low, b)
        table.append((steps, low))
        steps = (steps * 5) // 4
    return fourth(table)


def squaring_table():
    rho = (0.5 * CUBIC_TOLERANCE) ** 0.25
    top = 4.0 * rho / (1.0 + rho) ** 2
    table = []
    for count in range(1, 7):
        mu = top ** (0.5**count)
        table.append((count, 2.0 * mu / (1.0 - mu)))
    return fourth(table)


def fourth(table):
    return [(count, (limit / 1.001) ** 4) for count, limit in table]


def count_of(bound, table):
    count = table[0][0]
    for (_, limit), (more, _) in zip(table[:-1], table[1:]):
        count = jnp.where(bound > limit, more, count)
    return count


STEPS = step_table()
SQUARINGS = squaring_table()


def halves(a):
    high = a.astype(jnp.bfloat16)
    return high, (a - high.astype(jnp.float32)).astype(jnp.bfloat16)


def dots3(operands, dims):
    dot = lambda u, v: lax.dot_general(u, v, dims, preferred_element_type=jnp.float32)
    tops = [dot(a[0], b[0]) for a, b in operands]
    lows = [dot(a[0], b[1]) for a, b in operands]
    highs = [dot(a[1], b[0]) for a, b in operands]
    return [t + (l + h) for t, l, h in zip(tops, lows, highs)]


def slots_of(which):
    first_b = jnp.where(which == 0, 2, 1)
    second_b = jnp.where(which == 2, 2, 3)
    return ((0, which + 1), (first_b, second_b))


def pick(pairing_ref, step):
    row = pairing_ref[step : step + 1, :]
    mine = lax.broadcasted_iota(jnp.int32, row.shape, 1) == lax.axis_index(COL)
    return jnp.max(jnp.where(mine, row, 0).astype(jnp.float32)).astype(jnp.int32)


def load_blocks(refs, blocks):
    if len(refs) == 1:
        for s in range(4):
            blocks[s] = refs[0][:, s * WIDTH : (s + 1) * WIDTH]
    else:
        low, high, near, far = refs
        core = lax.axis_index(CORE)
        blocks[0] = low[...]
        blocks[2] = high[...]
        blocks[3 - 2 * core] = near[1 - core]
        blocks[1 + 2 * core] = far[...]


def fetch_gram_kernel(pairing_hbm, slab_hbm, out, blocks, pairing, slab, sems):
    copies = [
        pltpu.make_async_copy(pairing_hbm, pairing, sems.at[0]),
        pltpu.make_async_copy(slab_hbm, slab, sems.at[1]),
    ]
    for copy in copies:
        copy.start()
    for copy in copies:
        copy.wait()
    gram_kernel(0, pairing, slab, out, blocks)


def gram_kernel(step, pairing_ref, *refs):
    *ins, out, blocks = refs
    load_blocks(ins, blocks)
    norms = []
    for pair, (f, s) in enumerate(slots_of(pick(pairing_ref, step))):
        x = blocks[f]
        y = blocks[s]
        xh, xl = halves(x)
        yh, yl = halves(y)
        cross = lax.dot_general(
            jnp.concatenate([xh, xh, xl], axis=0),
            jnp.concatenate([yh, yl, yh], axis=0),
            TN,
            preferred_element_type=jnp.float32,
        )
        for block in (x, y):
            norm = jnp.sum(block * block, axis=0, keepdims=True)
            norms += [norm[:, :HALF], norm[:, HALF:]]
        for h in range(2):
            start = (2 * pair + h) * PART
            half = cross[:, h * HALF : (h + 1) * HALF]
            out[:, start : start + PART, :] = half.reshape(CHUNKS, PART, HALF)
    norms = jnp.concatenate(norms, axis=0)
    for c in range(CHUNKS):
        out[c, NORMS:] = norms


def sum_kernel(parts, out):
    total = parts[0]
    for c in range(1, parts.shape[0]):
        total = total + parts[c]
    for c in range(out.shape[0]):
        out[c] = total


def couple_kernel(parts, out, down):
    total = parts[0]
    for c in range(1, parts.shape[0]):
        total = total + parts[c]
    across = lax.rsqrt(total[NORMS:] + EPS)
    down[...] = across.T
    chunk = lax.axis_index(OUTER)
    half_chunks = CHUNKS // 2
    rows = down[pl.ds(pl.multiple_of(lax.rem(chunk, half_chunks) * PART, PART), PART), :]
    for pair in range(2):
        row = 4 * pair
        scale = jnp.where(chunk < half_chunks, rows[:, row : row + 1], rows[:, row + 1 : row + 2])
        for h in range(2):
            start = (2 * pair + h) * PART
            part = total[start : start + PART] * scale * across[row + 2 + h : row + 3 + h]
            for c in range(CHUNKS):
                out[c, start : start + PART] = part


def turn_kernel(step, pairing_ref, gram, *refs):
    count = 1 if step == 0 else 4
    ins, outs, (blocks, coupling, powers, solved) = refs[:count], refs[count:-4], refs[-4:]
    load_blocks(ins, blocks)
    pairs = slots_of(pick(pairing_ref, step))
    xs, ys, cs, ms, ts, starts, m_squares = [], [], [], [], [], [], []
    bound = None
    for pair, (f, s) in enumerate(pairs):
        x = blocks[f]
        y = blocks[s]
        sides = []
        for h in range(2):
            start = (2 * pair + h) * PART
            sides.append(gram[:, start : start + PART, :].reshape(WIDTH, HALF))
        coupling[pair] = jnp.concatenate(sides, axis=1)
        cs.append(halves(coupling[pair]))
        xs.append(x)
        ys.append(y)
    ms = dots3([(c, c) for c in cs], NT)
    ts = [x - yc for x, yc in zip(xs, dots3([(halves(y), c) for y, c in zip(ys, cs)], NT))]
    splits = [halves(m) for m in ms]
    m_squares = dots3([(m, m) for m in splits], NN)
    starts = dots3([(halves(t), m) for t, m in zip(ts, splits)], NN)
    for pair in range(2):
        most = jnp.sum(m_squares[pair] * m_squares[pair])
        bound = most if bound is None else jnp.maximum(bound, most)
    b = jnp.sqrt(jnp.sqrt(jnp.full((8, 128), bound, jnp.float32)))[:1, :1] * 1.001

    @pl.when(bound <= SQUARINGS[-1][1])
    def _():
        relax = 2.0 / (2.0 + b)
        keep = 0.5 * b * relax
        diagonal = lax.broadcasted_iota(jnp.int32, (WIDTH, WIDTH), 0) == lax.broadcasted_iota(
            jnp.int32, (WIDTH, WIDTH), 1
        )
        for pair in range(2):
            off = (relax * relax) * m_squares[pair] - (2.0 * keep * relax) * ms[pair]
            powers[pair] = jnp.where(diagonal, off + keep * keep, off)
            solved[pair] = relax * ((1.0 + keep) * ts[pair] - relax * starts[pair])

        def body(_, carry):
            zs = [solved[pair] for pair in range(2)]
            rs = [halves(powers[pair]) for pair in range(2)]
            zrs = dots3([(halves(z), r) for z, r in zip(zs, rs)], NN)
            squares = dots3([(r, r) for r in rs], NN)
            zs = [z + zr for z, zr in zip(zs, zrs)]
            for pair in range(2):
                solved[pair] = zs[pair]
                powers[pair] = squares[pair]
            return carry

        count = count_of(bound, SQUARINGS)
        lax.fori_loop(1, count, body, 0)
        top = keep
        for index in range(len(SQUARINGS)):
            top = jnp.where(count > index, top * top, top)
        third = 1.0
        second = third - 2.0 * top
        first = second + 1.25 * top * top
        zeroth = first - 0.25 * top * top * top
        unit = 1.0 / (zeroth + top * top * top * top * (1.0 / 128.0))
        zs = [solved[pair] for pair in range(2)]
        rs = [halves(powers[pair]) for pair in range(2)]
        squares = dots3([(r, r) for r in rs], NN)
        zrs = dots3([(halves(z), r) for z, r in zip(zs, rs)], NN)
        highs = [(unit * second) * z + unit * zr for z, zr in zip(zs, zrs)]
        tops = dots3([(halves(h), halves(q)) for h, q in zip(highs, squares)], NN)
        zs = [(unit * zeroth) * z + (unit * first) * zr + t for z, zr, t in zip(zs, zrs, tops)]
        zcs = dots3([(halves(z), c) for z, c in zip(zs, cs)], NN)
        for (f, s), x, y, z, zc in zip(pairs, xs, ys, zs, zcs):
            blocks[f] = 2.0 * z - x
            blocks[s] = y + 2.0 * zc

    @pl.when(bound > SQUARINGS[-1][1])
    def _():
        dot = functools.partial(
            lax.dot_general, precision=lax.Precision.HIGHEST, preferred_element_type=jnp.float32
        )
        relax = 2.0 / (2.0 + b)
        omega = 2.0 / (1.0 + relax * jnp.sqrt(1.0 + b))
        gain = omega * relax
        for pair, (f, s) in enumerate(pairs):
            x = blocks[f]
            y = blocks[s]
            c = coupling[pair]
            t = x - dot(y, c, NT)
            powers[pair] = dot(c, c, NT)

            def body(_, carry):
                z, before = carry
                residual = t - z - dot(z, powers[pair], NN)
                return before + omega * (z - before) + gain * residual, z

            z, _ = lax.fori_loop(0, count_of(bound, STEPS), body, (relax * t, jnp.zeros_like(t)))
            blocks[f] = 2.0 * z - x
            blocks[s] = y + 2.0 * dot(z, c, NN)

    if len(outs) == 1:
        for s in range(4):
            outs[0][:, s * WIDTH : (s + 1) * WIDTH] = blocks[s]
    else:
        low, high, near, far = outs
        core = lax.axis_index(CORE)
        low[...] = blocks[0]
        high[...] = blocks[2]
        near[0] = near[1] = blocks[1 + 2 * core]
        far[...] = blocks[3 - 2 * core]


VMEM = pl.BlockSpec(memory_space=pltpu.VMEM)
HBM = pl.BlockSpec(memory_space=pltpu.HBM)
BLOCKS = pltpu.VMEM((4, ROWS, WIDTH), jnp.float32)
PARAMS = pltpu.CompilerParams(vmem_limit_bytes=8 * 2**20)


def shape(*sizes):
    return jax.ShapeDtypeStruct(sizes, jnp.float32)


def first_gram(pairing, slab):
    return pl.pallas_call(
        fetch_gram_kernel,
        out_shape=shape(CHUNKS, NORMS + 8, HALF),
        in_specs=[HBM] * 2,
        out_specs=VMEM,
        scratch_shapes=[
            BLOCKS,
            pltpu.VMEM(pairing.shape, pairing.dtype),
            pltpu.VMEM(slab.shape, slab.dtype),
            pltpu.SemaphoreType.DMA((2,)),
        ],
        compiler_params=PARAMS,
        name="first_gram",
    )(pairing, slab)


def gram_of(step, pairing, ins):
    return pl.pallas_call(
        lambda *refs: gram_kernel(step, *refs),
        out_shape=shape(CHUNKS, NORMS + 8, HALF),
        in_specs=[VMEM] * (1 + len(ins)),
        out_specs=VMEM,
        scratch_shapes=[BLOCKS],
        compiler_params=PARAMS,
        name="gram",
    )(pairing, *ins)


def add_up(parts, copies):
    return pl.pallas_call(
        sum_kernel,
        out_shape=shape(copies, *parts.shape[1:]),
        in_specs=[VMEM],
        out_specs=VMEM,
        compiler_params=PARAMS,
        name="add_up",
    )(parts)


def couple(parts):
    return pl.pallas_call(
        couple_kernel,
        out_shape=shape(CHUNKS, NORMS, HALF),
        in_specs=[VMEM],
        out_specs=VMEM,
        scratch_shapes=[pltpu.VMEM((HALF, 8), jnp.float32)],
        compiler_params=PARAMS,
        name="couple",
    )(parts)


def turn(step, pairing, gram, ins):
    outs = [shape(ROWS, WIDTH)] * 2 + [shape(2, ROWS, WIDTH), shape(ROWS, WIDTH)] if step == 0 else shape(ROWS, 4 * WIDTH)
    return pl.pallas_call(
        lambda *refs: turn_kernel(step, *refs),
        out_shape=outs,
        in_specs=[VMEM] * (2 + len(ins)),
        out_specs=[VMEM] * 4 if step == 0 else VMEM,
        scratch_shapes=[
            BLOCKS,
            pltpu.VMEM((2, WIDTH, WIDTH), jnp.float32),
            pltpu.VMEM((2, WIDTH, WIDTH), jnp.float32),
            pltpu.VMEM((2, ROWS, WIDTH), jnp.float32),
        ],
        compiler_params=PARAMS,
        name="turn",
    )(pairing, gram, *ins)


def whole(parts):
    parts = add_up(lax.all_to_all(parts, OUTER, 0, 0), lax.axis_size(RING))
    parts = couple(lax.all_to_all(parts, RING, 0, 0))
    return lax.all_to_all(parts, OUTER, 0, 0)


def local(slab, pairing):
    ins = (slab,)
    gram = whole(first_gram(pltpu.with_memory_space_constraint(pairing, pltpu.HBM), pltpu.with_memory_space_constraint(slab, pltpu.HBM)))
    low, high, near, far = turn(0, pairing, gram, ins)
    far = lax.ppermute(far, COL, [(i, (i + 1 if i % 2 else i - 1) % 8) for i in range(8)])
    near = lax.all_to_all(near, CORE, 0, 0)
    ins = (low, high, near, far)
    gram = whole(gram_of(1, pairing, ins))
    return turn(1, pairing, gram, ins)


def solution(mesh):
    names = ("z_lo", "x", "y_hi", "y_lo", "z_hi", "core")
    fine = Mesh(mesh.devices.reshape(2, 4, 4, 2, 4, 2), names)
    spec = P(names[:4], COL)
    return jax.shard_map(local, mesh=fine, in_specs=(spec, P()), out_specs=spec, check_vma=False)
```

```python
import functools
import math

import jax
import jax.numpy as jnp
from jax import lax
from jax.experimental import pallas as pl
from jax.experimental.pallas import tpu as pltpu
from jax.sharding import Mesh, PartitionSpec as P

EPS = 1e-06
WIDTH = 256
HALF = 128
ROWS = 64
CHUNKS = 16
PART = 32
BANDS = WIDTH // PART
NORMS = 2 * PART
FULL = NORMS + 4
OUTER = ("z_lo", "x", "y_lo")
RING = ("y_hi",)
COL = ("z_hi", "core")
CORE = "core"

NT = (((1,), (1,)), ((), ()))
NN = (((1,), (0,)), ((), ()))
TN = (((0,), (0,)), ((), ()))


TOLERANCE = 2e-6
CLOSING_TOLERANCE = 1e-5


def step_table():
    table = []
    steps = 32
    while not table or table[-1][1] < 70000.0:
        low, high = 0.0, 1e6
        for _ in range(80):
            b = 0.5 * (low + high)
            root = 2.0 * math.sqrt(1.0 + b) / (2.0 + b)
            rho = b / (2.0 + b) / (1.0 + root)
            error = rho ** (steps + 1) * (1.0 + (steps + 1) * root)
            low, high = (b, high) if error < TOLERANCE else (low, b)
        table.append((steps, low))
        steps = (steps * 5) // 4
    return fourth(table)


def widest(degree):
    rho = (0.5 * CLOSING_TOLERANCE) ** (1.0 / (degree + 1))
    return 4.0 * rho / (1.0 + rho) ** 2


def squaring_table(degree):
    table = []
    for count in range(1, 6):
        mu = widest(degree) ** (0.5**count)
        table.append((count, 2.0 * mu / (1.0 - mu)))
    return fourth(table)


def fourth(table):
    return [(count, (limit / 1.001) ** 4) for count, limit in table]


def count_of(bound, table):
    count = table[0][0]
    for (_, limit), (more, _) in zip(table[:-1], table[1:]):
        count = jnp.where(bound > limit, more, count)
    return count


STEPS = step_table()
CUBIC = squaring_table(3)[0][1]
SQUARINGS = squaring_table(5)


def halves(a):
    high = a.astype(jnp.bfloat16)
    return high, (a - high.astype(jnp.float32)).astype(jnp.bfloat16)


def dots3(operands, dims):
    dot = lambda u, v: lax.dot_general(u, v, dims, preferred_element_type=jnp.float32)
    tops = [dot(a[0], b[0]) for a, b in operands]
    lows = [dot(a[0], b[1]) for a, b in operands]
    highs = [dot(a[1], b[0]) for a, b in operands]
    return [t + (l + h) for t, l, h in zip(tops, lows, highs)]


def slots_of(which):
    first_b = jnp.where(which == 0, 2, 1)
    second_b = jnp.where(which == 2, 2, 3)
    return ((0, which + 1), (first_b, second_b))


def pick(pairing_ref, step):
    row = pairing_ref[step : step + 1, :]
    mine = lax.broadcasted_iota(jnp.int32, row.shape, 1) == lax.axis_index(COL)
    return jnp.max(jnp.where(mine, row, 0).astype(jnp.float32)).astype(jnp.int32)


def load_blocks(refs, blocks):
    if len(refs) == 1:
        for s in range(4):
            blocks[s] = refs[0][:, s * WIDTH : (s + 1) * WIDTH]
    else:
        low, high, near, far = refs
        core = lax.axis_index(CORE)
        blocks[0] = low[...]
        blocks[2] = high[...]
        blocks[3 - 2 * core] = near[1 - core]
        blocks[1 + 2 * core] = far[...]


def fetch_gram_kernel(pairing_hbm, slab_hbm, out, blocks, pairing, slab, sems):
    copies = [
        pltpu.make_async_copy(pairing_hbm, pairing, sems.at[0]),
        pltpu.make_async_copy(slab_hbm, slab, sems.at[1]),
    ]
    for copy in copies:
        copy.start()
    for copy in copies:
        copy.wait()
    gram_kernel(0, pairing, slab, out, blocks)


def gram_kernel(step, pairing_ref, *refs):
    *ins, out, blocks = refs
    load_blocks(ins, blocks)
    norms = []
    for pair, (f, s) in enumerate(slots_of(pick(pairing_ref, step))):
        x = blocks[f]
        y = blocks[s]
        xh, xl = halves(x)
        yh, yl = halves(y)
        cross = lax.dot_general(
            jnp.concatenate([xh, xh, xl], axis=0),
            jnp.concatenate([yh, yl, yh], axis=0),
            TN,
            preferred_element_type=jnp.float32,
        )
        norms.append([jnp.sum(block * block, axis=0, keepdims=True) for block in (x, y)])
        for h in range(2):
            half = cross[:, h * HALF : (h + 1) * HALF].reshape(BANDS, PART, HALF)
            out[h * BANDS : (h + 1) * BANDS, pair * PART : (pair + 1) * PART, :] = half
    (xa, ya), (xb, yb) = norms
    for h in range(2):
        for g in range(2):
            columns = slice(h * HALF, (h + 1) * HALF)
            rows = slice(g * HALF, (g + 1) * HALF)
            tail = jnp.concatenate([ya[:, columns], yb[:, columns], xa[:, rows], xb[:, rows]], axis=0)
            for k in range(BANDS // 2):
                out[h * BANDS + g * (BANDS // 2) + k, NORMS:] = tail


def sum_kernel(parts, out):
    total = parts[0]
    for c in range(1, parts.shape[0]):
        total = total + parts[c]
    for c in range(out.shape[0]):
        out[c] = total


def couple_kernel(parts, out, down):
    total = parts[0]
    for c in range(1, parts.shape[0]):
        total = total + parts[c]
    across = lax.rsqrt(total[NORMS:] + EPS)
    down[...] = jnp.concatenate([across, across], axis=0).T
    start = pl.multiple_of(lax.rem(lax.axis_index(OUTER), HALF // PART) * PART, PART)
    rows = down[pl.ds(start, PART), :]
    for pair in range(2):
        part = total[pair * PART : (pair + 1) * PART]
        part = part * rows[:, 2 + pair : 3 + pair] * across[pair : pair + 1]
        for c in range(CHUNKS):
            out[c, pair * PART : (pair + 1) * PART] = part


def turn_kernel(step, pairing_ref, gram, *refs):
    count = 1 if step == 0 else 4
    ins, outs, (blocks, coupling, powers, solved) = refs[:count], refs[count:-4], refs[-4:]
    load_blocks(ins, blocks)
    pairs = slots_of(pick(pairing_ref, step))
    xs, ys, cs, ms, ts, starts, m_squares = [], [], [], [], [], [], []
    bound = None
    for pair, (f, s) in enumerate(pairs):
        x = blocks[f]
        y = blocks[s]
        sides = []
        for h in range(2):
            part = gram[h * BANDS : (h + 1) * BANDS, pair * PART : (pair + 1) * PART, :]
            sides.append(part.reshape(WIDTH, HALF))
        coupling[pair] = jnp.concatenate(sides, axis=1)
        cs.append(halves(coupling[pair]))
        xs.append(x)
        ys.append(y)
    ms = dots3([(c, c) for c in cs], NT)
    ts = [x - yc for x, yc in zip(xs, dots3([(halves(y), c) for y, c in zip(ys, cs)], NT))]
    splits = [halves(m) for m in ms]
    m_squares = dots3([(m, m) for m in splits], NN)
    starts = dots3([(halves(t), m) for t, m in zip(ts, splits)], NN)
    for pair in range(2):
        most = jnp.sum(m_squares[pair] * m_squares[pair])
        bound = most if bound is None else jnp.maximum(bound, most)
    b = jnp.sqrt(jnp.sqrt(jnp.full((8, 128), bound, jnp.float32)))[:1, :1] * 1.001

    @pl.when(bound <= SQUARINGS[-1][1])
    def _():
        relax = 2.0 / (2.0 + b)
        keep = 0.5 * b * relax
        diagonal = lax.broadcasted_iota(jnp.int32, (WIDTH, WIDTH), 0) == lax.broadcasted_iota(
            jnp.int32, (WIDTH, WIDTH), 1
        )
        for pair in range(2):
            off = (relax * relax) * m_squares[pair] - (2.0 * keep * relax) * ms[pair]
            powers[pair] = jnp.where(diagonal, off + keep * keep, off)
            solved[pair] = relax * ((1.0 + keep) * ts[pair] - relax * starts[pair])

        def body(_, carry):
            zs = [solved[pair] for pair in range(2)]
            rs = [halves(powers[pair]) for pair in range(2)]
            zrs = dots3([(halves(z), r) for z, r in zip(zs, rs)], NN)
            squares = dots3([(r, r) for r in rs], NN)
            zs = [z + zr for z, zr in zip(zs, zrs)]
            for pair in range(2):
                solved[pair] = zs[pair]
                powers[pair] = squares[pair]
            return carry

        count = count_of(bound, SQUARINGS)
        lax.fori_loop(1, count, body, 0)
        top = keep
        for index in range(len(SQUARINGS)):
            top = jnp.where(count > index, top * top, top)
        cubic = bound <= CUBIC
        top2 = top * top
        top3 = top2 * top
        top4 = top2 * top2
        zero = jnp.zeros_like(top)
        fifth = jnp.where(cubic, zero, zero + 1.0)
        fourth = jnp.where(cubic, zero, 1.0 - 3.0 * top)
        third = jnp.where(cubic, zero + 1.0, fourth + 3.375 * top2)
        second = third - jnp.where(cubic, 2.0 * top, 1.75 * top3)
        first = second + jnp.where(cubic, 1.25 * top2, 0.41015625 * top4)
        zeroth = first - jnp.where(cubic, 0.25 * top3, 0.03515625 * top4 * top)
        unit = 1.0 / (zeroth + jnp.where(cubic, top4 * (1.0 / 128.0), top4 * top2 * (1.0 / 2048.0)))
        zs = [solved[pair] for pair in range(2)]
        rs = [halves(powers[pair]) for pair in range(2)]
        squares = [halves(q) for q in dots3([(r, r) for r in rs], NN)]
        zrs = dots3([(halves(z), r) for z, r in zip(zs, rs)], NN)
        for pair in range(2):
            solved[pair] = (unit * second) * zs[pair] + (unit * third) * zrs[pair]

        @pl.when(jnp.logical_not(cubic))
        def _():
            highs = [(unit * fourth) * z + (unit * fifth) * zr for z, zr in zip(zs, zrs)]
            tops = dots3([(halves(h), q) for h, q in zip(highs, squares)], NN)
            for pair in range(2):
                solved[pair] += tops[pair]

        tops = dots3([(halves(solved[pair]), squares[pair]) for pair in range(2)], NN)
        zs = [(unit * zeroth) * z + (unit * first) * zr + t for z, zr, t in zip(zs, zrs, tops)]
        zcs = dots3([(halves(z), c) for z, c in zip(zs, cs)], NN)
        for (f, s), x, y, z, zc in zip(pairs, xs, ys, zs, zcs):
            blocks[f] = 2.0 * z - x
            blocks[s] = y + 2.0 * zc

    @pl.when(bound > SQUARINGS[-1][1])
    def _():
        dot = functools.partial(
            lax.dot_general, precision=lax.Precision.HIGHEST, preferred_element_type=jnp.float32
        )
        relax = 2.0 / (2.0 + b)
        omega = 2.0 / (1.0 + relax * jnp.sqrt(1.0 + b))
        gain = omega * relax
        for pair, (f, s) in enumerate(pairs):
            x = blocks[f]
            y = blocks[s]
            c = coupling[pair]
            t = x - dot(y, c, NT)
            powers[pair] = dot(c, c, NT)

            def body(_, carry):
                z, before = carry
                residual = t - z - dot(z, powers[pair], NN)
                return before + omega * (z - before) + gain * residual, z

            z, _ = lax.fori_loop(0, count_of(bound, STEPS), body, (relax * t, jnp.zeros_like(t)))
            blocks[f] = 2.0 * z - x
            blocks[s] = y + 2.0 * dot(z, c, NN)

    if len(outs) == 1:
        for s in range(4):
            outs[0][:, s * WIDTH : (s + 1) * WIDTH] = blocks[s]
    else:
        low, high, near, far = outs
        core = lax.axis_index(CORE)
        low[...] = blocks[0]
        high[...] = blocks[2]
        near[0] = near[1] = blocks[1 + 2 * core]
        far[...] = blocks[3 - 2 * core]


VMEM = pl.BlockSpec(memory_space=pltpu.VMEM)
HBM = pl.BlockSpec(memory_space=pltpu.HBM)
BLOCKS = pltpu.VMEM((4, ROWS, WIDTH), jnp.float32)
PARAMS = pltpu.CompilerParams(vmem_limit_bytes=8 * 2**20)


def shape(*sizes):
    return jax.ShapeDtypeStruct(sizes, jnp.float32)


def first_gram(pairing, slab):
    return pl.pallas_call(
        fetch_gram_kernel,
        out_shape=shape(CHUNKS, FULL, HALF),
        in_specs=[HBM] * 2,
        out_specs=VMEM,
        scratch_shapes=[
            BLOCKS,
            pltpu.VMEM(pairing.shape, pairing.dtype),
            pltpu.VMEM(slab.shape, slab.dtype),
            pltpu.SemaphoreType.DMA((2,)),
        ],
        compiler_params=PARAMS,
        name="first_gram",
    )(pairing, slab)


def gram_of(step, pairing, ins):
    return pl.pallas_call(
        lambda *refs: gram_kernel(step, *refs),
        out_shape=shape(CHUNKS, FULL, HALF),
        in_specs=[VMEM] * (1 + len(ins)),
        out_specs=VMEM,
        scratch_shapes=[BLOCKS],
        compiler_params=PARAMS,
        name="gram",
    )(pairing, *ins)


def add_up(parts, copies):
    return pl.pallas_call(
        sum_kernel,
        out_shape=shape(copies, *parts.shape[1:]),
        in_specs=[VMEM],
        out_specs=VMEM,
        compiler_params=PARAMS,
        name="add_up",
    )(parts)


def couple(parts):
    return pl.pallas_call(
        couple_kernel,
        out_shape=shape(CHUNKS, NORMS, HALF),
        in_specs=[VMEM],
        out_specs=VMEM,
        scratch_shapes=[pltpu.VMEM((HALF, 8), jnp.float32)],
        compiler_params=PARAMS,
        name="couple",
    )(parts)


def turn(step, pairing, gram, ins):
    outs = [shape(ROWS, WIDTH)] * 2 + [shape(2, ROWS, WIDTH), shape(ROWS, WIDTH)] if step == 0 else shape(ROWS, 4 * WIDTH)
    return pl.pallas_call(
        lambda *refs: turn_kernel(step, *refs),
        out_shape=outs,
        in_specs=[VMEM] * (2 + len(ins)),
        out_specs=[VMEM] * 4 if step == 0 else VMEM,
        scratch_shapes=[
            BLOCKS,
            pltpu.VMEM((2, WIDTH, WIDTH), jnp.float32),
            pltpu.VMEM((2, WIDTH, WIDTH), jnp.float32),
            pltpu.VMEM((2, ROWS, WIDTH), jnp.float32),
        ],
        compiler_params=PARAMS,
        name="turn",
    )(pairing, gram, *ins)


def whole(parts):
    parts = add_up(lax.all_to_all(parts, OUTER, 0, 0), lax.axis_size(RING))
    parts = couple(lax.all_to_all(parts, RING, 0, 0))
    return lax.all_to_all(parts, OUTER, 0, 0)


def local(slab, pairing):
    ins = (slab,)
    gram = whole(first_gram(pltpu.with_memory_space_constraint(pairing, pltpu.HBM), pltpu.with_memory_space_constraint(slab, pltpu.HBM)))
    low, high, near, far = turn(0, pairing, gram, ins)
    far = lax.ppermute(far, COL, [(i, (i + 1 if i % 2 else i - 1) % 8) for i in range(8)])
    near = lax.all_to_all(near, CORE, 0, 0)
    ins = (low, high, near, far)
    gram = whole(gram_of(1, pairing, ins))
    return turn(1, pairing, gram, ins)


def solution(mesh):
    names = ("z_lo", "x", "y_hi", "y_lo", "z_hi", "core")
    fine = Mesh(mesh.devices.reshape(2, 4, 4, 2, 4, 2), names)
    spec = P(names[:4], COL)
    return jax.shard_map(local, mesh=fine, in_specs=(spec, P()), out_specs=spec, check_vma=False)
```

```python
import functools
import math

import jax
import jax.numpy as jnp
from jax import lax
from jax.experimental import pallas as pl
from jax.experimental.pallas import tpu as pltpu
from jax.sharding import Mesh, PartitionSpec as P

EPS = 1e-06
WIDTH = 256
HALF = 128
ROWS = 64
CHUNKS = 16
PART = 32
BANDS = WIDTH // PART
NORMS = 2 * PART
FULL = NORMS + 4
OUTER = ("z_lo", "x", "y_lo")
RING = ("y_hi",)
COL = ("z_hi", "core")
CORE = "core"

NT = (((1,), (1,)), ((), ()))
NN = (((1,), (0,)), ((), ()))
TN = (((0,), (0,)), ((), ()))


TOLERANCE = 2e-6
CLOSING_TOLERANCE = 1e-5


def step_table():
    table = []
    steps = 32
    while not table or table[-1][1] < 70000.0:
        low, high = 0.0, 1e6
        for _ in range(80):
            b = 0.5 * (low + high)
            root = 2.0 * math.sqrt(1.0 + b) / (2.0 + b)
            rho = b / (2.0 + b) / (1.0 + root)
            error = rho ** (steps + 1) * (1.0 + (steps + 1) * root)
            low, high = (b, high) if error < TOLERANCE else (low, b)
        table.append((steps, low))
        steps = (steps * 5) // 4
    return fourth(table)


def widest(degree):
    rho = (0.5 * CLOSING_TOLERANCE) ** (1.0 / (degree + 1))
    return 4.0 * rho / (1.0 + rho) ** 2


def squaring_table(degree):
    table = []
    for count in range(1, 6):
        mu = widest(degree) ** (0.5**count)
        table.append((count, 2.0 * mu / (1.0 - mu)))
    return fourth(table)


def fourth(table):
    return [(count, (limit / 1.001) ** 4) for count, limit in table]


def count_of(bound, table):
    count = table[0][0]
    for (_, limit), (more, _) in zip(table[:-1], table[1:]):
        count = jnp.where(bound > limit, more, count)
    return count


STEPS = step_table()
CUBIC = squaring_table(3)[0][1]
SQUARINGS = squaring_table(5)


def halves(a):
    high = a.astype(jnp.bfloat16)
    return high, (a - high.astype(jnp.float32)).astype(jnp.bfloat16)


def dots3(operands, dims):
    dot = lambda u, v: lax.dot_general(u, v, dims, preferred_element_type=jnp.float32)
    rows = [a[0].shape[0] for a, _ in operands]
    both = [dot(jnp.concatenate(a, axis=0), b[0]) for a, b in operands]
    lows = [dot(a[0], b[1]) for a, b in operands]
    return [t[:r] + (l + t[r:]) for t, l, r in zip(both, lows, rows)]


def shared3(lefts, rights, dims):
    joined = [tuple(jnp.concatenate(p, axis=0) for p in zip(*ls)) for ls in lefts]
    products = dots3(list(zip(joined, rights)), dims)
    out = []
    for ls, product in zip(lefts, products):
        start, parts = 0, []
        for l in ls:
            parts.append(product[start : start + l[0].shape[0]])
            start += l[0].shape[0]
        out.append(parts)
    return out


def slots_of(which):
    first_b = jnp.where(which == 0, 2, 1)
    second_b = jnp.where(which == 2, 2, 3)
    return ((0, which + 1), (first_b, second_b))


def pick(pairing_ref, step):
    row = pairing_ref[step : step + 1, :]
    mine = lax.broadcasted_iota(jnp.int32, row.shape, 1) == lax.axis_index(COL)
    return jnp.max(jnp.where(mine, row, 0).astype(jnp.float32)).astype(jnp.int32)


def load_blocks(refs, blocks):
    if len(refs) == 1:
        for s in range(4):
            blocks[s] = refs[0][:, s * WIDTH : (s + 1) * WIDTH]
    else:
        low, high, near, far = refs
        core = lax.axis_index(CORE)
        blocks[0] = low[...]
        blocks[2] = high[...]
        blocks[3 - 2 * core] = near[1 - core]
        blocks[1 + 2 * core] = far[...]


def fetch_gram_kernel(pairing_hbm, slab_hbm, out, blocks, pairing, slab, sems):
    copies = [
        pltpu.make_async_copy(pairing_hbm, pairing, sems.at[0]),
        pltpu.make_async_copy(slab_hbm, slab, sems.at[1]),
    ]
    for copy in copies:
        copy.start()
    for copy in copies:
        copy.wait()
    gram_kernel(0, pairing, slab, out, blocks)


def gram_kernel(step, pairing_ref, *refs):
    *ins, out, blocks = refs
    load_blocks(ins, blocks)
    norms = []
    for pair, (f, s) in enumerate(slots_of(pick(pairing_ref, step))):
        x = blocks[f]
        y = blocks[s]
        xh, xl = halves(x)
        yh, yl = halves(y)
        cross = lax.dot_general(
            jnp.concatenate([xh, xh, xl], axis=0),
            jnp.concatenate([yh, yl, yh], axis=0),
            TN,
            preferred_element_type=jnp.float32,
        )
        norms.append([jnp.sum(block * block, axis=0, keepdims=True) for block in (x, y)])
        for h in range(2):
            for k in range(BANDS):
                start = (h * BANDS + k) * FULL + pair * PART
                out[start : start + PART, :] = cross[k * PART : (k + 1) * PART, h * HALF : (h + 1) * HALF]
    (xa, ya), (xb, yb) = norms
    for h in range(2):
        for g in range(2):
            columns = slice(h * HALF, (h + 1) * HALF)
            rows = slice(g * HALF, (g + 1) * HALF)
            tail = jnp.concatenate([ya[:, columns], yb[:, columns], xa[:, rows], xb[:, rows]], axis=0)
            for k in range(BANDS // 2):
                start = (h * BANDS + g * (BANDS // 2) + k) * FULL + NORMS
                out[start : start + FULL - NORMS, :] = tail


def total_of(parts):
    total = parts[:FULL]
    for start in range(FULL, parts.shape[0], FULL):
        total = total + parts[start : start + FULL]
    return total


def sum_kernel(parts, out):
    total = total_of(parts)
    for start in range(0, out.shape[0], FULL):
        out[start : start + FULL] = total


def couple_kernel(parts, out, down):
    total = total_of(parts)
    across = lax.rsqrt(total[NORMS:] + EPS)
    down[...] = jnp.concatenate([across, across], axis=0).T
    start = pl.multiple_of(lax.rem(lax.axis_index(OUTER), HALF // PART) * PART, PART)
    rows = down[pl.ds(start, PART), :]
    for pair in range(2):
        part = total[pair * PART : (pair + 1) * PART]
        part = part * rows[:, 2 + pair : 3 + pair] * across[pair : pair + 1]
        for c in range(CHUNKS):
            out[c, pair * PART : (pair + 1) * PART] = part


def turn_kernel(step, pairing_ref, gram, *refs):
    count = 1 if step == 0 else 4
    ins, outs, (blocks, coupling, powers, solved) = refs[:count], refs[count:-4], refs[-4:]
    load_blocks(ins, blocks)
    pairs = slots_of(pick(pairing_ref, step))
    xs, ys, cs, ms, ts, starts, m_squares = [], [], [], [], [], [], []
    bound = None
    for pair, (f, s) in enumerate(pairs):
        x = blocks[f]
        y = blocks[s]
        sides = []
        for h in range(2):
            part = gram[h * BANDS : (h + 1) * BANDS, pair * PART : (pair + 1) * PART, :]
            sides.append(part.reshape(WIDTH, HALF))
        coupling[pair] = jnp.concatenate(sides, axis=1)
        cs.append(halves(coupling[pair]))
        xs.append(x)
        ys.append(y)
    ms = dots3([(c, c) for c in cs], NT)
    ts = [x - yc for x, yc in zip(xs, dots3([(halves(y), c) for y, c in zip(ys, cs)], NT))]
    splits = [halves(m) for m in ms]
    m_squares = dots3([(m, m) for m in splits], NN)
    starts = dots3([(halves(t), m) for t, m in zip(ts, splits)], NN)
    for pair in range(2):
        most = jnp.sum(m_squares[pair] * m_squares[pair])
        bound = most if bound is None else jnp.maximum(bound, most)
    b = jnp.sqrt(jnp.sqrt(jnp.full((8, 128), bound, jnp.float32)))[:1, :1] * 1.001

    @pl.when(bound <= SQUARINGS[-1][1])
    def _():
        relax = 2.0 / (2.0 + b)
        keep = 0.5 * b * relax
        diagonal = lax.broadcasted_iota(jnp.int32, (WIDTH, WIDTH), 0) == lax.broadcasted_iota(
            jnp.int32, (WIDTH, WIDTH), 1
        )
        for pair in range(2):
            off = (relax * relax) * m_squares[pair] - (2.0 * keep * relax) * ms[pair]
            powers[pair] = jnp.where(diagonal, off + keep * keep, off)
            solved[pair] = relax * ((1.0 + keep) * ts[pair] - relax * starts[pair])

        def body(_, carry):
            zs = [solved[pair] for pair in range(2)]
            rs = [halves(powers[pair]) for pair in range(2)]
            zrs = dots3([(halves(z), r) for z, r in zip(zs, rs)], NN)
            squares = dots3([(r, r) for r in rs], NN)
            zs = [z + zr for z, zr in zip(zs, zrs)]
            for pair in range(2):
                solved[pair] = zs[pair]
                powers[pair] = squares[pair]
            return carry

        count = count_of(bound, SQUARINGS)
        lax.fori_loop(1, count, body, 0)
        top = keep
        for index in range(len(SQUARINGS)):
            top = jnp.where(count > index, top * top, top)
        cubic = bound <= CUBIC
        top2 = top * top
        top3 = top2 * top
        top4 = top2 * top2
        zero = jnp.zeros_like(top)
        fifth = jnp.where(cubic, zero, zero + 1.0)
        fourth = jnp.where(cubic, zero, 1.0 - 3.0 * top)
        third = jnp.where(cubic, zero + 1.0, fourth + 3.375 * top2)
        second = third - jnp.where(cubic, 2.0 * top, 1.75 * top3)
        first = second + jnp.where(cubic, 1.25 * top2, 0.41015625 * top4)
        zeroth = first - jnp.where(cubic, 0.25 * top3, 0.03515625 * top4 * top)
        unit = 1.0 / (zeroth + jnp.where(cubic, top4 * (1.0 / 128.0), top4 * top2 * (1.0 / 2048.0)))
        zs = [solved[pair] for pair in range(2)]
        rs = [halves(powers[pair]) for pair in range(2)]
        squares = [halves(q) for q in dots3([(r, r) for r in rs], NN)]
        zrs = dots3([(halves(z), r) for z, r in zip(zs, rs)], NN)
        for pair in range(2):
            solved[pair] = (unit * second) * zs[pair] + (unit * third) * zrs[pair]

        @pl.when(jnp.logical_not(cubic))
        def _():
            highs = [(unit * fourth) * z + (unit * fifth) * zr for z, zr in zip(zs, zrs)]
            tops = dots3([(halves(h), q) for h, q in zip(highs, squares)], NN)
            for pair in range(2):
                solved[pair] += tops[pair]

        tops = dots3([(halves(solved[pair]), squares[pair]) for pair in range(2)], NN)
        zs = [(unit * zeroth) * z + (unit * first) * zr + t for z, zr, t in zip(zs, zrs, tops)]
        zcs = dots3([(halves(z), c) for z, c in zip(zs, cs)], NN)
        for (f, s), x, y, z, zc in zip(pairs, xs, ys, zs, zcs):
            blocks[f] = 2.0 * z - x
            blocks[s] = y + 2.0 * zc

    @pl.when(bound > SQUARINGS[-1][1])
    def _():
        dot = functools.partial(
            lax.dot_general, precision=lax.Precision.HIGHEST, preferred_element_type=jnp.float32
        )
        relax = 2.0 / (2.0 + b)
        omega = 2.0 / (1.0 + relax * jnp.sqrt(1.0 + b))
        gain = omega * relax
        for pair, (f, s) in enumerate(pairs):
            x = blocks[f]
            y = blocks[s]
            c = coupling[pair]
            t = x - dot(y, c, NT)
            powers[pair] = dot(c, c, NT)

            def body(_, carry):
                z, before = carry
                residual = t - z - dot(z, powers[pair], NN)
                return before + omega * (z - before) + gain * residual, z

            z, _ = lax.fori_loop(0, count_of(bound, STEPS), body, (relax * t, jnp.zeros_like(t)))
            blocks[f] = 2.0 * z - x
            blocks[s] = y + 2.0 * dot(z, c, NN)

    if len(outs) == 1:
        for s in range(4):
            outs[0][:, s * WIDTH : (s + 1) * WIDTH] = blocks[s]
    else:
        low, high, near, far = outs
        core = lax.axis_index(CORE)
        low[...] = blocks[0]
        high[...] = blocks[2]
        near[0] = near[1] = blocks[1 + 2 * core]
        far[...] = blocks[3 - 2 * core]


VMEM = pl.BlockSpec(memory_space=pltpu.VMEM)
HBM = pl.BlockSpec(memory_space=pltpu.HBM)
BLOCKS = pltpu.VMEM((4, ROWS, WIDTH), jnp.float32)
PARAMS = pltpu.CompilerParams(vmem_limit_bytes=8 * 2**20)


def shape(*sizes):
    return jax.ShapeDtypeStruct(sizes, jnp.float32)


def first_gram(pairing, slab):
    return pl.pallas_call(
        fetch_gram_kernel,
        out_shape=shape(CHUNKS * FULL, HALF),
        in_specs=[HBM] * 2,
        out_specs=VMEM,
        scratch_shapes=[
            BLOCKS,
            pltpu.VMEM(pairing.shape, pairing.dtype),
            pltpu.VMEM(slab.shape, slab.dtype),
            pltpu.SemaphoreType.DMA((2,)),
        ],
        compiler_params=PARAMS,
        name="first_gram",
    )(pairing, slab)


def gram_of(step, pairing, ins):
    return pl.pallas_call(
        lambda *refs: gram_kernel(step, *refs),
        out_shape=shape(CHUNKS * FULL, HALF),
        in_specs=[VMEM] * (1 + len(ins)),
        out_specs=VMEM,
        scratch_shapes=[BLOCKS],
        compiler_params=PARAMS,
        name="gram",
    )(pairing, *ins)


def add_up(parts, copies):
    return pl.pallas_call(
        sum_kernel,
        out_shape=shape(copies * FULL, HALF),
        in_specs=[VMEM],
        out_specs=VMEM,
        compiler_params=PARAMS,
        name="add_up",
    )(parts)


def couple(parts):
    return pl.pallas_call(
        couple_kernel,
        out_shape=shape(CHUNKS, NORMS, HALF),
        in_specs=[VMEM],
        out_specs=VMEM,
        scratch_shapes=[pltpu.VMEM((HALF, 8), jnp.float32)],
        compiler_params=PARAMS,
        name="couple",
    )(parts)


def turn(step, pairing, gram, ins):
    outs = [shape(ROWS, WIDTH)] * 2 + [shape(2, ROWS, WIDTH), shape(ROWS, WIDTH)] if step == 0 else shape(ROWS, 4 * WIDTH)
    return pl.pallas_call(
        lambda *refs: turn_kernel(step, *refs),
        out_shape=outs,
        in_specs=[VMEM] * (2 + len(ins)),
        out_specs=[VMEM] * 4 if step == 0 else VMEM,
        scratch_shapes=[
            BLOCKS,
            pltpu.VMEM((2, WIDTH, WIDTH), jnp.float32),
            pltpu.VMEM((2, WIDTH, WIDTH), jnp.float32),
            pltpu.VMEM((2, ROWS, WIDTH), jnp.float32),
        ],
        compiler_params=PARAMS,
        name="turn",
    )(pairing, gram, *ins)


def exchange(parts, axes):
    count = lax.axis_size(axes)
    parts = lax.all_to_all(parts.reshape(count, FULL // 4, 4, HALF), axes, 0, 0)
    return parts.reshape(count * FULL, HALF)


def whole(parts):
    parts = add_up(exchange(parts, OUTER), lax.axis_size(RING))
    return lax.all_to_all(couple(exchange(parts, RING)), OUTER, 0, 0)


def local(slab, pairing):
    ins = (slab,)
    gram = whole(first_gram(pltpu.with_memory_space_constraint(pairing, pltpu.HBM), pltpu.with_memory_space_constraint(slab, pltpu.HBM)))
    low, high, near, far = turn(0, pairing, gram, ins)
    far = lax.ppermute(far, COL, [(i, (i + 1 if i % 2 else i - 1) % 8) for i in range(8)])
    near = lax.all_to_all(near, CORE, 0, 0)
    ins = (low, high, near, far)
    gram = whole(gram_of(1, pairing, ins))
    return turn(1, pairing, gram, ins)


def solution(mesh):
    names = ("z_lo", "x", "y_hi", "y_lo", "z_hi", "core")
    fine = Mesh(mesh.devices.reshape(2, 4, 4, 2, 4, 2), names)
    spec = P(names[:4], COL)
    return jax.shard_map(local, mesh=fine, in_specs=(spec, P()), out_specs=spec, check_vma=False)
```

```python
import functools
import math

import jax
import jax.numpy as jnp
from jax import lax
from jax.experimental import pallas as pl
from jax.experimental.pallas import tpu as pltpu
from jax.sharding import Mesh, PartitionSpec as P

EPS = 1e-06
WIDTH = 256
HALF = 128
ROWS = 64
CHUNKS = 16
PART = 32
BANDS = WIDTH // PART
NORMS = 2 * PART
FULL = NORMS + 4
OUTER = ("x", "z_lo", "y_lo")
RING = ("y_hi",)
COL = ("z_hi", "core")
CORE = "core"

NT = (((1,), (1,)), ((), ()))
NN = (((1,), (0,)), ((), ()))
TN = (((0,), (0,)), ((), ()))


TOLERANCE = 2e-6
CLOSING_TOLERANCE = 1e-5


def step_table():
    table = []
    steps = 32
    while not table or table[-1][1] < 70000.0:
        low, high = 0.0, 1e6
        for _ in range(80):
            b = 0.5 * (low + high)
            root = 2.0 * math.sqrt(1.0 + b) / (2.0 + b)
            rho = b / (2.0 + b) / (1.0 + root)
            error = rho ** (steps + 1) * (1.0 + (steps + 1) * root)
            low, high = (b, high) if error < TOLERANCE else (low, b)
        table.append((steps, low))
        steps = (steps * 5) // 4
    return fourth(table)


def widest(degree):
    rho = (0.5 * CLOSING_TOLERANCE) ** (1.0 / (degree + 1))
    return 4.0 * rho / (1.0 + rho) ** 2


def squaring_table(degree):
    table = []
    for count in range(1, 6):
        mu = widest(degree) ** (0.5**count)
        table.append((count, 2.0 * mu / (1.0 - mu)))
    return fourth(table)


def fourth(table):
    return [(count, (limit / 1.001) ** 4) for count, limit in table]


def count_of(bound, table):
    count = table[0][0]
    for (_, limit), (more, _) in zip(table[:-1], table[1:]):
        count = jnp.where(bound > limit, more, count)
    return count


STEPS = step_table()
CUBIC = squaring_table(3)[0][1]
SQUARINGS = squaring_table(5)


def halves(a):
    high = a.astype(jnp.bfloat16)
    return high, (a - high.astype(jnp.float32)).astype(jnp.bfloat16)


def dots3(operands, dims):
    dot = lambda u, v: lax.dot_general(u, v, dims, preferred_element_type=jnp.float32)
    rows = [a[0].shape[0] for a, _ in operands]
    both = [dot(jnp.concatenate(a, axis=0), b[0]) for a, b in operands]
    lows = [dot(a[0], b[1]) for a, b in operands]
    return [t[:r] + (l + t[r:]) for t, l, r in zip(both, lows, rows)]


def shared3(lefts, rights, dims):
    joined = [tuple(jnp.concatenate(p, axis=0) for p in zip(*ls)) for ls in lefts]
    products = dots3(list(zip(joined, rights)), dims)
    out = []
    for ls, product in zip(lefts, products):
        start, parts = 0, []
        for l in ls:
            parts.append(product[start : start + l[0].shape[0]])
            start += l[0].shape[0]
        out.append(parts)
    return out


def slots_of(which):
    first_b = jnp.where(which == 0, 2, 1)
    second_b = jnp.where(which == 2, 2, 3)
    return ((0, which + 1), (first_b, second_b))


def pick(pairing_ref, step):
    row = pairing_ref[step : step + 1, :]
    mine = lax.broadcasted_iota(jnp.int32, row.shape, 1) == lax.axis_index(COL)
    return jnp.max(jnp.where(mine, row, 0).astype(jnp.float32)).astype(jnp.int32)


def load_blocks(refs, blocks):
    if len(refs) == 1:
        for s in range(4):
            blocks[s] = refs[0][:, s * WIDTH : (s + 1) * WIDTH]
    else:
        low, high, near, far = refs
        core = lax.axis_index(CORE)
        blocks[0] = low[...]
        blocks[2] = high[...]
        blocks[3 - 2 * core] = near[1 - core]
        blocks[1 + 2 * core] = far[...]


def fetch_gram_kernel(pairing_hbm, slab_hbm, out, blocks, pairing, slab, sems):
    copies = [
        pltpu.make_async_copy(pairing_hbm, pairing, sems.at[0]),
        pltpu.make_async_copy(slab_hbm, slab, sems.at[1]),
    ]
    for copy in copies:
        copy.start()
    for copy in copies:
        copy.wait()
    gram_kernel(0, pairing, slab, out, blocks)


def gram_kernel(step, pairing_ref, *refs):
    *ins, out, blocks = refs
    load_blocks(ins, blocks)
    norms = []
    for pair, (f, s) in enumerate(slots_of(pick(pairing_ref, step))):
        x = blocks[f]
        y = blocks[s]
        xh, xl = halves(x)
        yh, yl = halves(y)
        cross = lax.dot_general(
            jnp.concatenate([xh, xh, xl], axis=0),
            jnp.concatenate([yh, yl, yh], axis=0),
            TN,
            preferred_element_type=jnp.float32,
        )
        norms.append([jnp.sum(block * block, axis=0, keepdims=True) for block in (x, y)])
        for h in range(2):
            for k in range(BANDS):
                start = (h * BANDS + k) * FULL + pair * PART
                out[start : start + PART, :] = cross[k * PART : (k + 1) * PART, h * HALF : (h + 1) * HALF]
    (xa, ya), (xb, yb) = norms
    for h in range(2):
        for g in range(2):
            columns = slice(h * HALF, (h + 1) * HALF)
            rows = slice(g * HALF, (g + 1) * HALF)
            tail = jnp.concatenate([ya[:, columns], yb[:, columns], xa[:, rows], xb[:, rows]], axis=0)
            for k in range(BANDS // 2):
                start = (h * BANDS + g * (BANDS // 2) + k) * FULL + NORMS
                out[start : start + FULL - NORMS, :] = tail


def total_of(parts):
    total = parts[:FULL]
    for start in range(FULL, parts.shape[0], FULL):
        total = total + parts[start : start + FULL]
    return total


def sum_kernel(parts, out):
    total = total_of(parts)
    for start in range(0, out.shape[0], FULL):
        out[start : start + FULL] = total


def couple_kernel(parts, out, down):
    total = total_of(parts)
    across = lax.rsqrt(total[NORMS:] + EPS)
    down[...] = jnp.concatenate([across, across], axis=0).T
    start = pl.multiple_of(lax.rem(lax.axis_index(OUTER), HALF // PART) * PART, PART)
    rows = down[pl.ds(start, PART), :]
    for pair in range(2):
        part = total[pair * PART : (pair + 1) * PART]
        part = part * rows[:, 2 + pair : 3 + pair] * across[pair : pair + 1]
        for c in range(CHUNKS):
            out[c, pair * PART : (pair + 1) * PART] = part


def turn_kernel(step, pairing_ref, gram, *refs):
    count = 1 if step == 0 else 4
    ins, outs, (blocks, coupling, powers, solved) = refs[:count], refs[count:-4], refs[-4:]
    load_blocks(ins, blocks)
    pairs = slots_of(pick(pairing_ref, step))
    xs, ys, cs, ms, ts, starts, m_squares = [], [], [], [], [], [], []
    bound = None
    for pair, (f, s) in enumerate(pairs):
        x = blocks[f]
        y = blocks[s]
        sides = []
        for h in range(2):
            part = gram[h * BANDS : (h + 1) * BANDS, pair * PART : (pair + 1) * PART, :]
            sides.append(part.reshape(WIDTH, HALF))
        coupling[pair] = jnp.concatenate(sides, axis=1)
        cs.append(halves(coupling[pair]))
        xs.append(x)
        ys.append(y)
    ms = dots3([(c, c) for c in cs], NT)
    ts = [x - yc for x, yc in zip(xs, dots3([(halves(y), c) for y, c in zip(ys, cs)], NT))]
    splits = [halves(m) for m in ms]
    m_squares = dots3([(m, m) for m in splits], NN)
    starts = dots3([(halves(t), m) for t, m in zip(ts, splits)], NN)
    for pair in range(2):
        most = jnp.sum(m_squares[pair] * m_squares[pair])
        bound = most if bound is None else jnp.maximum(bound, most)
    b = jnp.sqrt(jnp.sqrt(jnp.full((8, 128), bound, jnp.float32)))[:1, :1] * 1.001

    @pl.when(bound <= SQUARINGS[-1][1])
    def _():
        relax = 2.0 / (2.0 + b)
        keep = 0.5 * b * relax
        diagonal = lax.broadcasted_iota(jnp.int32, (WIDTH, WIDTH), 0) == lax.broadcasted_iota(
            jnp.int32, (WIDTH, WIDTH), 1
        )
        for pair in range(2):
            off = (relax * relax) * m_squares[pair] - (2.0 * keep * relax) * ms[pair]
            powers[pair] = jnp.where(diagonal, off + keep * keep, off)
            solved[pair] = relax * ((1.0 + keep) * ts[pair] - relax * starts[pair])

        def body(_, carry):
            zs = [solved[pair] for pair in range(2)]
            rs = [halves(powers[pair]) for pair in range(2)]
            zrs = dots3([(halves(z), r) for z, r in zip(zs, rs)], NN)
            squares = dots3([(r, r) for r in rs], NN)
            zs = [z + zr for z, zr in zip(zs, zrs)]
            for pair in range(2):
                solved[pair] = zs[pair]
                powers[pair] = squares[pair]
            return carry

        count = count_of(bound, SQUARINGS)
        lax.fori_loop(1, count, body, 0)
        top = keep
        for index in range(len(SQUARINGS)):
            top = jnp.where(count > index, top * top, top)
        cubic = bound <= CUBIC
        top2 = top * top
        top3 = top2 * top
        top4 = top2 * top2
        zero = jnp.zeros_like(top)
        fifth = jnp.where(cubic, zero, zero + 1.0)
        fourth = jnp.where(cubic, zero, 1.0 - 3.0 * top)
        third = jnp.where(cubic, zero + 1.0, fourth + 3.375 * top2)
        second = third - jnp.where(cubic, 2.0 * top, 1.75 * top3)
        first = second + jnp.where(cubic, 1.25 * top2, 0.41015625 * top4)
        zeroth = first - jnp.where(cubic, 0.25 * top3, 0.03515625 * top4 * top)
        unit = 1.0 / (zeroth + jnp.where(cubic, top4 * (1.0 / 128.0), top4 * top2 * (1.0 / 2048.0)))
        zs = [solved[pair] for pair in range(2)]
        rs = [halves(powers[pair]) for pair in range(2)]
        squares = [halves(q) for q in dots3([(r, r) for r in rs], NN)]
        zrs = dots3([(halves(z), r) for z, r in zip(zs, rs)], NN)
        for pair in range(2):
            solved[pair] = (unit * second) * zs[pair] + (unit * third) * zrs[pair]

        @pl.when(jnp.logical_not(cubic))
        def _():
            highs = [(unit * fourth) * z + (unit * fifth) * zr for z, zr in zip(zs, zrs)]
            tops = dots3([(halves(h), q) for h, q in zip(highs, squares)], NN)
            for pair in range(2):
                solved[pair] += tops[pair]

        tops = dots3([(halves(solved[pair]), squares[pair]) for pair in range(2)], NN)
        zs = [(unit * zeroth) * z + (unit * first) * zr + t for z, zr, t in zip(zs, zrs, tops)]
        zcs = dots3([(halves(z), c) for z, c in zip(zs, cs)], NN)
        for (f, s), x, y, z, zc in zip(pairs, xs, ys, zs, zcs):
            blocks[f] = 2.0 * z - x
            blocks[s] = y + 2.0 * zc

    @pl.when(bound > SQUARINGS[-1][1])
    def _():
        dot = functools.partial(
            lax.dot_general, precision=lax.Precision.HIGHEST, preferred_element_type=jnp.float32
        )
        relax = 2.0 / (2.0 + b)
        omega = 2.0 / (1.0 + relax * jnp.sqrt(1.0 + b))
        gain = omega * relax
        for pair, (f, s) in enumerate(pairs):
            x = blocks[f]
            y = blocks[s]
            c = coupling[pair]
            t = x - dot(y, c, NT)
            powers[pair] = dot(c, c, NT)

            def body(_, carry):
                z, before = carry
                residual = t - z - dot(z, powers[pair], NN)
                return before + omega * (z - before) + gain * residual, z

            z, _ = lax.fori_loop(0, count_of(bound, STEPS), body, (relax * t, jnp.zeros_like(t)))
            blocks[f] = 2.0 * z - x
            blocks[s] = y + 2.0 * dot(z, c, NN)

    if len(outs) == 1:
        for s in range(4):
            outs[0][:, s * WIDTH : (s + 1) * WIDTH] = blocks[s]
    else:
        low, high, near, far = outs
        core = lax.axis_index(CORE)
        low[...] = blocks[0]
        high[...] = blocks[2]
        near[0] = near[1] = blocks[1 + 2 * core]
        far[...] = blocks[3 - 2 * core]


VMEM = pl.BlockSpec(memory_space=pltpu.VMEM)
HBM = pl.BlockSpec(memory_space=pltpu.HBM)
BLOCKS = pltpu.VMEM((4, ROWS, WIDTH), jnp.float32)
PARAMS = pltpu.CompilerParams(vmem_limit_bytes=8 * 2**20)


def shape(*sizes):
    return jax.ShapeDtypeStruct(sizes, jnp.float32)


def first_gram(pairing, slab):
    return pl.pallas_call(
        fetch_gram_kernel,
        out_shape=shape(CHUNKS * FULL, HALF),
        in_specs=[HBM] * 2,
        out_specs=VMEM,
        scratch_shapes=[
            BLOCKS,
            pltpu.VMEM(pairing.shape, pairing.dtype),
            pltpu.VMEM(slab.shape, slab.dtype),
            pltpu.SemaphoreType.DMA((2,)),
        ],
        compiler_params=PARAMS,
        name="first_gram",
    )(pairing, slab)


def gram_of(step, pairing, ins):
    return pl.pallas_call(
        lambda *refs: gram_kernel(step, *refs),
        out_shape=shape(CHUNKS * FULL, HALF),
        in_specs=[VMEM] * (1 + len(ins)),
        out_specs=VMEM,
        scratch_shapes=[BLOCKS],
        compiler_params=PARAMS,
        name="gram",
    )(pairing, *ins)


def add_up(parts, copies):
    return pl.pallas_call(
        sum_kernel,
        out_shape=shape(copies * FULL, HALF),
        in_specs=[VMEM],
        out_specs=VMEM,
        compiler_params=PARAMS,
        name="add_up",
    )(parts)


def couple(parts):
    return pl.pallas_call(
        couple_kernel,
        out_shape=shape(CHUNKS, NORMS, HALF),
        in_specs=[VMEM],
        out_specs=VMEM,
        scratch_shapes=[pltpu.VMEM((HALF, 8), jnp.float32)],
        compiler_params=PARAMS,
        name="couple",
    )(parts)


def turn(step, pairing, gram, ins):
    outs = [shape(ROWS, WIDTH)] * 2 + [shape(2, ROWS, WIDTH), shape(ROWS, WIDTH)] if step == 0 else shape(ROWS, 4 * WIDTH)
    return pl.pallas_call(
        lambda *refs: turn_kernel(step, *refs),
        out_shape=outs,
        in_specs=[VMEM] * (2 + len(ins)),
        out_specs=[VMEM] * 4 if step == 0 else VMEM,
        scratch_shapes=[
            BLOCKS,
            pltpu.VMEM((2, WIDTH, WIDTH), jnp.float32),
            pltpu.VMEM((2, WIDTH, WIDTH), jnp.float32),
            pltpu.VMEM((2, ROWS, WIDTH), jnp.float32),
        ],
        compiler_params=PARAMS,
        name="turn",
    )(pairing, gram, *ins)


def exchange(parts, axes):
    count = lax.axis_size(axes)
    parts = lax.all_to_all(parts.reshape(count, FULL // 4, 4, HALF), axes, 0, 0)
    return parts.reshape(count * FULL, HALF)


def whole(parts):
    parts = add_up(exchange(parts, OUTER), lax.axis_size(RING))
    return lax.all_to_all(couple(exchange(parts, RING)), OUTER, 0, 0)


def local(slab, pairing):
    ins = (slab,)
    gram = whole(first_gram(pltpu.with_memory_space_constraint(pairing, pltpu.HBM), pltpu.with_memory_space_constraint(slab, pltpu.HBM)))
    low, high, near, far = turn(0, pairing, gram, ins)
    far = lax.ppermute(far, COL, [(i, (i + 1 if i % 2 else i - 1) % 8) for i in range(8)])
    near = lax.all_to_all(near, CORE, 0, 0)
    ins = (low, high, near, far)
    gram = whole(gram_of(1, pairing, ins))
    return turn(1, pairing, gram, ins)


def solution(mesh):
    names = ("z_lo", "x", "y_hi", "y_lo", "z_hi", "core")
    fine = Mesh(mesh.devices.reshape(2, 4, 4, 2, 4, 2), names)
    spec = P(names[:4], COL)
    return jax.shard_map(local, mesh=fine, in_specs=(spec, P()), out_specs=spec, check_vma=False)
```

```python
import functools
import math

import jax
import jax.numpy as jnp
from jax import lax
from jax.experimental import pallas as pl
from jax.experimental.pallas import tpu as pltpu
from jax.sharding import Mesh, PartitionSpec as P

EPS = 1e-06
WIDTH = 256
HALF = 128
ROWS = 64
CHUNKS = 16
PART = 32
BANDS = WIDTH // PART
NORMS = 2 * PART
FULL = NORMS + 4
OUTER = ("x", "z_lo", "y_lo")
RING = ("y_hi",)
COL = ("z_hi", "core")
CORE = "core"

NT = (((1,), (1,)), ((), ()))
NN = (((1,), (0,)), ((), ()))
TN = (((0,), (0,)), ((), ()))


TOLERANCE = 2e-6
CLOSING_TOLERANCE = 1e-5


def step_table():
    table = []
    steps = 32
    while not table or table[-1][1] < 70000.0:
        low, high = 0.0, 1e6
        for _ in range(80):
            b = 0.5 * (low + high)
            root = 2.0 * math.sqrt(1.0 + b) / (2.0 + b)
            rho = b / (2.0 + b) / (1.0 + root)
            error = rho ** (steps + 1) * (1.0 + (steps + 1) * root)
            low, high = (b, high) if error < TOLERANCE else (low, b)
        table.append((steps, low))
        steps = (steps * 5) // 4
    return fourth(table)


def widest(degree):
    rho = (0.5 * CLOSING_TOLERANCE) ** (1.0 / (degree + 1))
    return 4.0 * rho / (1.0 + rho) ** 2


def squaring_table(degree):
    table = []
    for count in range(1, 6):
        mu = widest(degree) ** (0.5**count)
        table.append((count, 2.0 * mu / (1.0 - mu)))
    return fourth(table)


def fourth(table):
    return [(count, (limit / 1.001) ** 4) for count, limit in table]


def count_of(bound, table):
    count = table[0][0]
    for (_, limit), (more, _) in zip(table[:-1], table[1:]):
        count = jnp.where(bound > limit, more, count)
    return count


STEPS = step_table()
CUBIC = squaring_table(3)[0][1]
SQUARINGS = squaring_table(5)


def halves(a):
    high = a.astype(jnp.bfloat16)
    return high, (a - high.astype(jnp.float32)).astype(jnp.bfloat16)


def dots3(operands, dims):
    dot = lambda u, v: lax.dot_general(u, v, dims, preferred_element_type=jnp.float32)
    rows = [a[0].shape[0] for a, _ in operands]
    both = [dot(jnp.concatenate(a, axis=0), b[0]) for a, b in operands]
    lows = [dot(a[0], b[1]) for a, b in operands]
    return [t[:r] + (l + t[r:]) for t, l, r in zip(both, lows, rows)]


def shared3(lefts, rights, dims):
    joined = [tuple(jnp.concatenate(p, axis=0) for p in zip(*ls)) for ls in lefts]
    products = dots3(list(zip(joined, rights)), dims)
    out = []
    for ls, product in zip(lefts, products):
        start, parts = 0, []
        for l in ls:
            parts.append(product[start : start + l[0].shape[0]])
            start += l[0].shape[0]
        out.append(parts)
    return out


def slots_of(which):
    first_b = jnp.where(which == 0, 2, 1)
    second_b = jnp.where(which == 2, 2, 3)
    return ((0, which + 1), (first_b, second_b))


def pick(pairing_ref, step):
    row = pairing_ref[step : step + 1, :]
    mine = lax.broadcasted_iota(jnp.int32, row.shape, 1) == lax.axis_index(COL)
    return jnp.max(jnp.where(mine, row, 0).astype(jnp.float32)).astype(jnp.int32)


def load_blocks(refs, blocks):
    if len(refs) == 1:
        for s in range(4):
            blocks[s] = refs[0][:, s * WIDTH : (s + 1) * WIDTH]
    else:
        low, high, near, far = refs
        core = lax.axis_index(CORE)
        blocks[0] = low[...]
        blocks[2] = high[...]
        blocks[3 - 2 * core] = near[1 - core]
        blocks[1 + 2 * core] = far[...]


def fetch_gram_kernel(pairing_hbm, slab_hbm, out, blocks, pairing, slab, sems):
    copies = [
        pltpu.make_async_copy(pairing_hbm, pairing, sems.at[0]),
        pltpu.make_async_copy(slab_hbm, slab, sems.at[1]),
    ]
    for copy in copies:
        copy.start()
    for copy in copies:
        copy.wait()
    write_gram(pairing[0, lax.axis_index(COL)], (slab,), out, blocks)


def gram_kernel(step, pairing_ref, *refs):
    *ins, out, blocks = refs
    write_gram(pick(pairing_ref, step), ins, out, blocks)


def write_gram(which, ins, out, blocks):
    load_blocks(ins, blocks)
    norms = []
    for pair, (f, s) in enumerate(slots_of(which)):
        x = blocks[f]
        y = blocks[s]
        xh, xl = halves(x)
        yh, yl = halves(y)
        cross = lax.dot_general(
            jnp.concatenate([xh, xh, xl], axis=0),
            jnp.concatenate([yh, yl, yh], axis=0),
            TN,
            preferred_element_type=jnp.float32,
        )
        norms.append([jnp.sum(block * block, axis=0, keepdims=True) for block in (x, y)])
        for h in range(2):
            for k in range(BANDS):
                start = (h * BANDS + k) * FULL + pair * PART
                out[start : start + PART, :] = cross[k * PART : (k + 1) * PART, h * HALF : (h + 1) * HALF]
    (xa, ya), (xb, yb) = norms
    for h in range(2):
        for g in range(2):
            columns = slice(h * HALF, (h + 1) * HALF)
            rows = slice(g * HALF, (g + 1) * HALF)
            tail = jnp.concatenate([ya[:, columns], yb[:, columns], xa[:, rows], xb[:, rows]], axis=0)
            for k in range(BANDS // 2):
                start = (h * BANDS + g * (BANDS // 2) + k) * FULL + NORMS
                out[start : start + FULL - NORMS, :] = tail


def total_of(parts):
    total = parts[:FULL]
    for start in range(FULL, parts.shape[0], FULL):
        total = total + parts[start : start + FULL]
    return total


def sum_kernel(parts, out):
    total = total_of(parts)
    for start in range(0, out.shape[0], FULL):
        out[start : start + FULL] = total


def couple_kernel(parts, out, down):
    total = total_of(parts)
    across = lax.rsqrt(total[NORMS:] + EPS)
    down[...] = jnp.concatenate([across, across], axis=0).T
    start = pl.multiple_of(lax.rem(lax.axis_index(OUTER), HALF // PART) * PART, PART)
    rows = down[pl.ds(start, PART), :]
    for pair in range(2):
        part = total[pair * PART : (pair + 1) * PART]
        part = part * rows[:, 2 + pair : 3 + pair] * across[pair : pair + 1]
        for c in range(CHUNKS):
            out[c, pair * PART : (pair + 1) * PART] = part


def turn_kernel(step, pairing_ref, gram, *refs):
    count = 1 if step == 0 else 4
    ins, outs, (blocks, coupling, powers, solved, done, sems) = refs[:count], refs[count:-6], refs[-6:]
    load_blocks(ins, blocks)

    def finish(pair, side, slot, value):
        if step == 0:
            blocks[slot] = value
            return []
        index = 2 * pair + side
        done[index] = value
        dest = outs[0].at[:, pl.ds(pl.multiple_of(slot * WIDTH, WIDTH), WIDTH)]
        copy = pltpu.make_async_copy(done.at[index], dest, sems.at[index])
        copy.start()
        return [copy]

    pairs = slots_of(pick(pairing_ref, step))
    xs, ys, cs, ms, ts, starts, m_squares = [], [], [], [], [], [], []
    bound = None
    for pair, (f, s) in enumerate(pairs):
        x = blocks[f]
        y = blocks[s]
        sides = []
        for h in range(2):
            part = gram[h * BANDS : (h + 1) * BANDS, pair * PART : (pair + 1) * PART, :]
            sides.append(part.reshape(WIDTH, HALF))
        coupling[pair] = jnp.concatenate(sides, axis=1)
        cs.append(halves(coupling[pair]))
        xs.append(x)
        ys.append(y)
    ms = dots3([(c, c) for c in cs], NT)
    ts = [x - yc for x, yc in zip(xs, dots3([(halves(y), c) for y, c in zip(ys, cs)], NT))]
    splits = [halves(m) for m in ms]
    m_squares = dots3([(m, m) for m in splits], NN)
    starts = dots3([(halves(t), m) for t, m in zip(ts, splits)], NN)
    for pair in range(2):
        most = jnp.sum(m_squares[pair] * m_squares[pair])
        bound = most if bound is None else jnp.maximum(bound, most)
    b = jnp.sqrt(jnp.sqrt(jnp.full((8, 128), bound, jnp.float32)))[:1, :1] * 1.001

    @pl.when(bound <= SQUARINGS[-1][1])
    def _():
        relax = 2.0 / (2.0 + b)
        keep = 0.5 * b * relax
        diagonal = lax.broadcasted_iota(jnp.int32, (WIDTH, WIDTH), 0) == lax.broadcasted_iota(
            jnp.int32, (WIDTH, WIDTH), 1
        )
        for pair in range(2):
            off = (relax * relax) * m_squares[pair] - (2.0 * keep * relax) * ms[pair]
            powers[pair] = jnp.where(diagonal, off + keep * keep, off)
            solved[pair] = relax * ((1.0 + keep) * ts[pair] - relax * starts[pair])

        def body(_, carry):
            zs = [solved[pair] for pair in range(2)]
            rs = [halves(powers[pair]) for pair in range(2)]
            zrs = dots3([(halves(z), r) for z, r in zip(zs, rs)], NN)
            squares = dots3([(r, r) for r in rs], NN)
            zs = [z + zr for z, zr in zip(zs, zrs)]
            for pair in range(2):
                solved[pair] = zs[pair]
                powers[pair] = squares[pair]
            return carry

        count = count_of(bound, SQUARINGS)
        lax.fori_loop(1, count, body, 0)
        top = keep
        for index in range(len(SQUARINGS)):
            top = jnp.where(count > index, top * top, top)
        cubic = bound <= CUBIC
        top2 = top * top
        top3 = top2 * top
        top4 = top2 * top2
        zero = jnp.zeros_like(top)
        fifth = jnp.where(cubic, zero, zero + 1.0)
        fourth = jnp.where(cubic, zero, 1.0 - 3.0 * top)
        third = jnp.where(cubic, zero + 1.0, fourth + 3.375 * top2)
        second = third - jnp.where(cubic, 2.0 * top, 1.75 * top3)
        first = second + jnp.where(cubic, 1.25 * top2, 0.41015625 * top4)
        zeroth = first - jnp.where(cubic, 0.25 * top3, 0.03515625 * top4 * top)
        unit = 1.0 / (zeroth + jnp.where(cubic, top4 * (1.0 / 128.0), top4 * top2 * (1.0 / 2048.0)))
        zs = [solved[pair] for pair in range(2)]
        rs = [halves(powers[pair]) for pair in range(2)]
        squares = [halves(q) for q in dots3([(r, r) for r in rs], NN)]
        zrs = dots3([(halves(z), r) for z, r in zip(zs, rs)], NN)
        for pair in range(2):
            solved[pair] = (unit * second) * zs[pair] + (unit * third) * zrs[pair]

        @pl.when(jnp.logical_not(cubic))
        def _():
            highs = [(unit * fourth) * z + (unit * fifth) * zr for z, zr in zip(zs, zrs)]
            tops = dots3([(halves(h), q) for h, q in zip(highs, squares)], NN)
            for pair in range(2):
                solved[pair] += tops[pair]

        tops = dots3([(halves(solved[pair]), squares[pair]) for pair in range(2)], NN)
        zs = [(unit * zeroth) * z + (unit * first) * zr + t for z, zr, t in zip(zs, zrs, tops)]
        copies = []
        for pair, (f, _) in enumerate(pairs):
            copies += finish(pair, 0, f, 2.0 * zs[pair] - xs[pair])
        zcs = dots3([(halves(z), c) for z, c in zip(zs, cs)], NN)
        for pair, (_, s) in enumerate(pairs):
            copies += finish(pair, 1, s, ys[pair] + 2.0 * zcs[pair])
        for copy in copies:
            copy.wait()

    @pl.when(bound > SQUARINGS[-1][1])
    def _():
        dot = functools.partial(
            lax.dot_general, precision=lax.Precision.HIGHEST, preferred_element_type=jnp.float32
        )
        relax = 2.0 / (2.0 + b)
        omega = 2.0 / (1.0 + relax * jnp.sqrt(1.0 + b))
        gain = omega * relax
        copies = []
        for pair, (f, s) in enumerate(pairs):
            x = blocks[f]
            y = blocks[s]
            c = coupling[pair]
            t = x - dot(y, c, NT)
            powers[pair] = dot(c, c, NT)

            def body(_, carry):
                z, before = carry
                residual = t - z - dot(z, powers[pair], NN)
                return before + omega * (z - before) + gain * residual, z

            z, _ = lax.fori_loop(0, count_of(bound, STEPS), body, (relax * t, jnp.zeros_like(t)))
            copies += finish(pair, 0, f, 2.0 * z - x)
            copies += finish(pair, 1, s, y + 2.0 * dot(z, c, NN))
        for copy in copies:
            copy.wait()

    if step == 0:
        low, high, near, far = outs
        core = lax.axis_index(CORE)
        low[...] = blocks[0]
        high[...] = blocks[2]
        near[0] = near[1] = blocks[1 + 2 * core]
        far[...] = blocks[3 - 2 * core]


VMEM = pl.BlockSpec(memory_space=pltpu.VMEM)
HBM = pl.BlockSpec(memory_space=pltpu.HBM)
BLOCKS = pltpu.VMEM((4, ROWS, WIDTH), jnp.float32)
PARAMS = pltpu.CompilerParams(vmem_limit_bytes=8 * 2**20)


def shape(*sizes):
    return jax.ShapeDtypeStruct(sizes, jnp.float32)


def first_gram(pairing, slab):
    return pl.pallas_call(
        fetch_gram_kernel,
        out_shape=shape(CHUNKS * FULL, HALF),
        in_specs=[HBM] * 2,
        out_specs=VMEM,
        scratch_shapes=[
            BLOCKS,
            pltpu.SMEM(pairing.shape, pairing.dtype),
            pltpu.VMEM(slab.shape, slab.dtype),
            pltpu.SemaphoreType.DMA((2,)),
        ],
        compiler_params=PARAMS,
        name="first_gram",
    )(pairing, slab)


def gram_of(step, pairing, ins):
    return pl.pallas_call(
        lambda *refs: gram_kernel(step, *refs),
        out_shape=shape(CHUNKS * FULL, HALF),
        in_specs=[VMEM] * (1 + len(ins)),
        out_specs=VMEM,
        scratch_shapes=[BLOCKS],
        compiler_params=PARAMS,
        name="gram",
    )(pairing, *ins)


def add_up(parts, copies):
    return pl.pallas_call(
        sum_kernel,
        out_shape=shape(copies * FULL, HALF),
        in_specs=[VMEM],
        out_specs=VMEM,
        compiler_params=PARAMS,
        name="add_up",
    )(parts)


def couple(parts):
    return pl.pallas_call(
        couple_kernel,
        out_shape=shape(CHUNKS, NORMS, HALF),
        in_specs=[VMEM],
        out_specs=VMEM,
        scratch_shapes=[pltpu.VMEM((HALF, 8), jnp.float32)],
        compiler_params=PARAMS,
        name="couple",
    )(parts)


def turn(step, pairing, gram, ins):
    outs = [shape(ROWS, WIDTH)] * 2 + [shape(2, ROWS, WIDTH), shape(ROWS, WIDTH)] if step == 0 else shape(ROWS, 4 * WIDTH)
    return pl.pallas_call(
        lambda *refs: turn_kernel(step, *refs),
        out_shape=outs,
        in_specs=[VMEM] * (2 + len(ins)),
        out_specs=[VMEM] * 4 if step == 0 else HBM,
        scratch_shapes=[
            BLOCKS,
            pltpu.VMEM((2, WIDTH, WIDTH), jnp.float32),
            pltpu.VMEM((2, WIDTH, WIDTH), jnp.float32),
            pltpu.VMEM((2, ROWS, WIDTH), jnp.float32),
            BLOCKS,
            pltpu.SemaphoreType.DMA((4,)),
        ],
        compiler_params=PARAMS,
        name="turn",
    )(pairing, gram, *ins)


def exchange(parts, axes):
    count = lax.axis_size(axes)
    parts = lax.all_to_all(parts.reshape(count, FULL // 4, 4, HALF), axes, 0, 0)
    return parts.reshape(count * FULL, HALF)


def whole(parts):
    parts = add_up(exchange(parts, OUTER), lax.axis_size(RING))
    return lax.all_to_all(couple(exchange(parts, RING)), OUTER, 0, 0)


def local(slab, pairing):
    ins = (slab,)
    gram = whole(first_gram(pltpu.with_memory_space_constraint(pairing, pltpu.HBM), pltpu.with_memory_space_constraint(slab, pltpu.HBM)))
    low, high, near, far = turn(0, pairing, gram, ins)
    far = lax.ppermute(far, COL, [(i, (i + 1 if i % 2 else i - 1) % 8) for i in range(8)])
    near = lax.all_to_all(near, CORE, 0, 0)
    ins = (low, high, near, far)
    gram = whole(gram_of(1, pairing, ins))
    return turn(1, pairing, gram, ins)


def solution(mesh):
    names = ("z_lo", "x", "y_hi", "y_lo", "z_hi", "core")
    fine = Mesh(mesh.devices.reshape(2, 4, 4, 2, 4, 2), names)
    spec = P(names[:4], COL)
    return jax.shard_map(local, mesh=fine, in_specs=(spec, P()), out_specs=spec, check_vma=False)
```
